32 devices in a mesh: ctx: 8 (over z, core), fsdp: 4 (over y, x).
Axes of the slice: x: 2, y: 2, z: 4, core: 2. Of those that a mesh axis runs over, the one named last changes fastest.
Arguments:
- tokens: bfloat16 [4, 8, 2, 64, 2560], P('fsdp', 'ctx'), may hold values from -6 to 6
- doc_starts: int32 [4, 8, 2, 64], P('fsdp', 'ctx'), may hold values from 0 to 1023, as said below
- gain_one: bfloat16 [2560], P('fsdp'), may hold values from 0.25 to 1.75
- w_query: bfloat16 [2560, 2560], P('fsdp'), may hold values from -0.15625 to 0.15625
- key_weight_matrix: bfloat16 [2560, 640], P('fsdp'), may hold values from -0.15625 to 0.15625
- value_weight_matrix: bfloat16 [2560, 640], P('fsdp'), may hold values from -0.125 to 0.125
- w_out: bfloat16 [2560, 2560], P('fsdp'), may hold values from -0.5 to 0.5
- gain_two: bfloat16 [2560], P('fsdp'), may hold values from 0.25 to 1.75
- w_gate: bfloat16 [2560, 7168], P('fsdp'), may hold values from -0.125 to 0.125
- w_up: bfloat16 [2560, 7168], P('fsdp'), may hold values from -0.125 to 0.125
- w_down: bfloat16 [7168, 2560], P('fsdp'), may hold values from -0.09375 to 0.09375
- cotangent: bfloat16 [4, 8, 2, 64, 2560], P('fsdp', 'ctx'), may hold values from -6 to 6
Outputs:
- mixed: float32 [4, 8, 2, 64, 2560], P('fsdp', 'ctx')
- grad_tokens: float32 [4, 8, 2, 64, 2560], P('fsdp', 'ctx')
- grad_gain_one: float32 [2560], P('fsdp')
- grad_w_query: float32 [2560, 2560], P('fsdp')
- grad_w_key: float32 [2560, 640], P('fsdp')
- grad_w_value: float32 [2560, 640], P('fsdp')
- grad_w_out: float32 [2560, 2560], P('fsdp')
- grad_gain_two: float32 [2560], P('fsdp')
- grad_w_gate: float32 [2560, 7168], P('fsdp')
- grad_w_up: float32 [2560, 7168], P('fsdp')
- grad_w_down: float32 [7168, 2560], P('fsdp')
The draws below stay inside these ranges and needn't reach their ends.
Inputs may be any that keep to these rules, and one draw needn't show every extreme that they name: `doc_starts`: documents are contiguous runs of a stream; each is at most 512 tokens and each stream has one of exactly 512 tokens.
All inputs are finite; a program needn't handle non-finite values.
Results may differ from the reference program's by a relative error of at most 0.025.
Values may be sent and summed in bfloat16 or wider, within the bound.
No kernel may reach another device: no remote copies, remote signals or barrier semaphores. Data moves between devices by JAX's collectives and lax.ppermute only.
A program may use at most 640 MiB of HBM per device.

```python
import jax
import jax.numpy as jnp
from jax import lax

MODEL_DIMENSION = 2560
QUERY_HEADS = 32
KEY_VALUE_HEADS = 8
HEAD_SIZE = 80
FF = 7168
BLOCK_LEN = 64
STREAM = 1024
STREAMS = 4
N_CTX = 8


def draw_doc_starts(key, part):
    key = jax.random.fold_in(key, 7)
    side_key, mark_key = jax.random.split(key)
    half_len = STREAM // 2
    side_pick = jax.random.randint(side_key, (STREAMS, 1), 0, 2)
    mark_draw = jax.random.randint(mark_key, (STREAMS, STREAM), 0, max(2, STREAM // 16))
    places = jnp.broadcast_to(jnp.arange(STREAM, dtype=jnp.int32)[None, :], (STREAMS, STREAM))
    ragged_low = jnp.where(side_pick == 0, half_len, 0)
    inside = (places >= ragged_low) & (places < ragged_low + half_len)
    bounds = inside & ((mark_draw == 0) | (places == ragged_low))
    latest = lax.cummax(jnp.where(bounds, places, -1), axis=1)
    long_start = jnp.where(side_pick == 0, 0, half_len)
    starts = jnp.where(inside, latest, long_start)
    blocks = starts.reshape(STREAMS, 2 * N_CTX, BLOCK_LEN)
    return jnp.stack([blocks[:, :N_CTX], blocks[:, N_CTX:][:, ::-1]], axis=2).astype(jnp.int32)


def level_of(key, shape, pieces, smallest, high):
    factor_of = 1.0
    for dim, parts in pieces:
        steps = jax.random.uniform(jax.random.fold_in(jax.random.fold_in(key, 6), dim), (parts,), jnp.float32, smallest / len(pieces), high / len(pieces))
        factor_of = factor_of * jnp.repeat(jnp.exp(steps), shape[dim] // parts).reshape((-1,) + (1,) * (len(shape) - 1 - dim))
    return factor_of


def normal_values(own_key, dims, scale, bound, pieces=(), kind=jnp.bfloat16):
    result = scale * jax.random.normal(own_key, dims, jnp.float32)
    if pieces:
        result = result * level_of(own_key, dims, pieces, -0.22, 0.18)
    return jnp.clip(result, -bound, bound).astype(kind)


def setup_inputs(seed: int = 0) -> dict:
    splits = jax.random.split(jax.random.key(seed), 13)
    tokens = normal_values(splits[0], (STREAMS, N_CTX, 2, BLOCK_LEN, MODEL_DIMENSION), 1.0, 6.0, ((0, 4), (1, 8)))
    doc_starts = draw_doc_starts(jax.random.fold_in(splits[12], 71), 0)
    gain_one = jnp.clip(1.0 + 0.15 * jax.random.normal(splits[2], (MODEL_DIMENSION,), jnp.float32), 0.25, 1.75).astype(jnp.bfloat16)
    w_query = normal_values(splits[3], (MODEL_DIMENSION, QUERY_HEADS * HEAD_SIZE), (MODEL_DIMENSION // 2) ** -0.5, 0.15625, ((0, 4),))
    key_weight_matrix = normal_values(splits[4], (MODEL_DIMENSION, KEY_VALUE_HEADS * HEAD_SIZE), (MODEL_DIMENSION // 2) ** -0.5, 0.15625, ((0, 4),))
    value_weight_matrix = normal_values(splits[5], (MODEL_DIMENSION, KEY_VALUE_HEADS * HEAD_SIZE), MODEL_DIMENSION ** -0.5, 0.125, ((0, 4),))
    w_out = normal_values(splits[6], (QUERY_HEADS * HEAD_SIZE, MODEL_DIMENSION), (MODEL_DIMENSION // 16) ** -0.5, 0.5, ((0, 4),))
    gain_two = jnp.clip(1.0 + 0.15 * jax.random.normal(splits[7], (MODEL_DIMENSION,), jnp.float32), 0.25, 1.75).astype(jnp.bfloat16)
    w_gate = normal_values(splits[8], (MODEL_DIMENSION, FF), MODEL_DIMENSION ** -0.5, 0.125, ((0, 4),))
    w_up = normal_values(splits[9], (MODEL_DIMENSION, FF), MODEL_DIMENSION ** -0.5, 0.125, ((0, 4),))
    w_down = normal_values(splits[10], (FF, MODEL_DIMENSION), (FF // 2) ** -0.5, 0.09375, ((0, 4),))
    cotangent = normal_values(splits[11], (STREAMS, N_CTX, 2, BLOCK_LEN, MODEL_DIMENSION), 1.0, 6.0, ((0, 4), (1, 8)))
    return dict(tokens=tokens, doc_starts=doc_starts, gain_one=gain_one, w_query=w_query, key_weight_matrix=key_weight_matrix, value_weight_matrix=value_weight_matrix, w_out=w_out, gain_two=gain_two, w_gate=w_gate, w_up=w_up, w_down=w_down, cotangent=cotangent)


@jax.custom_vjp
def reduced_precision(v):
    return lax.optimization_barrier(v.astype(jnp.bfloat16)).astype(jnp.float32)

@jax.custom_vjp
def reduced_precision_back(v):
    return v

def low_keep(v):
    return (reduced_precision(v), None)

def low_pass(kept, grad):
    return (grad,)

def back_keep(v):
    return (v, None)

def back_low(kept, grad):
    return (reduced_precision(grad),)
reduced_precision.defvjp(low_keep, low_pass)
reduced_precision_back.defvjp(back_keep, back_low)
EPS = 1e-05
THETA = 1000000.0
NEGATIVE_LARGE = -1e+30
HIGH = lax.Precision.HIGHEST

def matrix_product(left, right):
    return jnp.dot(left, right, precision=HIGH)

def rms_norm(values, norm_gain):
    inverse = lax.rsqrt(lax.optimization_barrier(jnp.mean(values * values, axis=-1, keepdims=True)) + EPS)
    return values * inverse * norm_gain

def apply_rotation(values, cosine_table, sine_table):
    half_dim = values.shape[-1] // 2
    lead_half = values[..., :half_dim]
    tail_half = values[..., half_dim:]
    return jnp.concatenate([lead_half * cosine_table - tail_half * sine_table, tail_half * cosine_table + lead_half * sine_table], axis=-1)

def to_stream(array):
    lead_rows = array[:, :, 0]
    tail_rows = array[:, ::-1, 1]
    both = jnp.concatenate([lead_rows, tail_rows], axis=1)
    return both.reshape((array.shape[0], STREAM) + array.shape[4:])

def from_stream(array):
    blocks = array.reshape((array.shape[0], 2 * N_CTX, BLOCK_LEN) + array.shape[2:])
    return jnp.stack([blocks[:, :N_CTX], blocks[:, N_CTX:][:, ::-1]], axis=2)

def stream_layer(weight_set, token_rows, starts):
    gain_one, w_query, key_weight_matrix, value_weight_matrix, w_out, gain_two, w_gate, w_up, w_down = weight_set
    sequence_length = token_rows.shape[0]
    query_group_width = QUERY_HEADS // KEY_VALUE_HEADS
    q_block = min(512, sequence_length)
    places = jnp.arange(sequence_length, dtype=jnp.int32)
    rel_pos = (places - starts).astype(jnp.float32)
    inv_freq = THETA ** (-(jnp.arange(HEAD_SIZE // 2, dtype=jnp.float32) * 2.0) / HEAD_SIZE)
    angles = rel_pos[:, None] * inv_freq[None, :]
    cosine_table = jnp.cos(angles)[:, None, :]
    sine_table = jnp.sin(angles)[:, None, :]
    first_normalized = reduced_precision(rms_norm(token_rows, gain_one))
    query_projected = reduced_precision_back(matrix_product(first_normalized, w_query)).reshape(sequence_length, QUERY_HEADS, HEAD_SIZE)
    key_projected = reduced_precision_back(matrix_product(first_normalized, key_weight_matrix)).reshape(sequence_length, KEY_VALUE_HEADS, HEAD_SIZE)
    value_row_matrix = reduced_precision(reduced_precision_back(matrix_product(first_normalized, value_weight_matrix))).reshape(sequence_length, KEY_VALUE_HEADS, HEAD_SIZE)
    query_matrix = reduced_precision(apply_rotation(query_projected, cosine_table, sine_table) * HEAD_SIZE ** (-0.5)).reshape(sequence_length, KEY_VALUE_HEADS, query_group_width, HEAD_SIZE)
    keys = reduced_precision(apply_rotation(key_projected, cosine_table, sine_table))

    def block_fn(block_index):
        q_rows = lax.dynamic_slice_in_dim(query_matrix, block_index * q_block, q_block, 0)
        q_pos = lax.dynamic_slice_in_dim(places, block_index * q_block, q_block, 0)
        q_start = lax.dynamic_slice_in_dim(starts, block_index * q_block, q_block, 0)
        scores = reduced_precision_back(jnp.einsum('qhgd,khd->hgqk', q_rows, keys, precision=HIGH))
        visible = (places[None, :] >= q_start[:, None]) & (places[None, :] <= q_pos[:, None])
        masked = jnp.where(visible, scores, NEGATIVE_LARGE)
        row_max = lax.optimization_barrier(jnp.max(masked, axis=-1, keepdims=True))
        exp_terms = jnp.where(visible, jnp.exp(masked - row_max), 0.0)
        probs = reduced_precision(exp_terms / lax.optimization_barrier(jnp.sum(exp_terms, axis=-1, keepdims=True)))
        outputs = jnp.einsum('hgqk,khd->qhgd', probs, value_row_matrix, precision=HIGH)
        return outputs.reshape(q_block, QUERY_HEADS * HEAD_SIZE)
    attn_rows = lax.map(jax.checkpoint(block_fn), jnp.arange(sequence_length // q_block, dtype=jnp.int32))
    attn_low = reduced_precision(reduced_precision_back(attn_rows.reshape(sequence_length, QUERY_HEADS * HEAD_SIZE)))
    middle = token_rows + reduced_precision_back(matrix_product(attn_low, w_out))
    normed_two = reduced_precision(rms_norm(middle, gain_two))
    gate_proj = reduced_precision_back(matrix_product(normed_two, w_gate))
    up_proj = reduced_precision_back(matrix_product(normed_two, w_up))
    hidden = reduced_precision(jax.nn.silu(gate_proj) * up_proj)
    return middle + reduced_precision_back(matrix_product(hidden, w_down))

def reference(tokens, doc_starts, gain_one, w_query, key_weight_matrix, value_weight_matrix, w_out, gain_two, w_gate, w_up, w_down, cotangent):
    weights = tuple((weight_in.astype(jnp.float32) for weight_in in (gain_one, w_query, key_weight_matrix, value_weight_matrix, w_out, gain_two, w_gate, w_up, w_down)))
    stream_tokens = to_stream(tokens.astype(jnp.float32))
    stream_starts = to_stream(doc_starts).astype(jnp.int32)

    def forward(token_rows, weight_set):
        return lax.map(lambda stream_pair: stream_layer(weight_set, stream_pair[0], stream_pair[1]), (token_rows, stream_starts))
    mixed, pullback = jax.vjp(forward, stream_tokens, weights)
    grad_rows, grad_weights = pullback(to_stream(cotangent.astype(jnp.float32)))
    grad_g1, grad_wq, grad_wk, grad_wv, grad_wo, grad_g2, grad_wg, grad_wu, grad_wd = grad_weights
    return (from_stream(mixed), from_stream(grad_rows), grad_g1, grad_wq, grad_wk, grad_wv, grad_wo, grad_g2, grad_wg, grad_wu, grad_wd)
```

```python
import jax
import jax.numpy as jnp
import numpy as np
from jax import lax
from jax.experimental import pallas as pl
from jax.experimental.pallas import tpu as pltpu
from jax.sharding import Mesh
from jax.sharding import PartitionSpec as P

QUERY_HEADS = 32
KEY_VALUE_HEADS = 8
HEAD_SIZE = 80
GROUP = QUERY_HEADS // KEY_VALUE_HEADS

EPS = 1e-05
THETA = 1000000.0
NEGATIVE_LARGE = -1e30

F32 = jnp.float32
BF16 = jnp.bfloat16


def after(value, *earlier):
    return lax.optimization_barrier((value,) + earlier)[0]


ANY = pl.BlockSpec(memory_space=pl.ANY)
VMEM_LIMIT = 56 * 1024 * 1024


def blank(shape, dtype):
    return pl.pallas_call(
        lambda out: None, out_shape=jax.ShapeDtypeStruct(shape, dtype), out_specs=ANY
    )()


def place(pieces, order):
    count = len(pieces)
    shape = pieces[0].shape

    def body(where, *refs):
        for i in range(count):

            @pl.when(pl.program_id(0) == i)
            def _(i=i):
                refs[count][0] = refs[i][...]

    zeros = (0,) * len(shape)
    return pl.pallas_call(
        body,
        out_shape=jax.ShapeDtypeStruct((count,) + shape, pieces[0].dtype),
        grid_spec=pltpu.PrefetchScalarGridSpec(
            num_scalar_prefetch=1,
            grid=(count,),
            in_specs=[pl.BlockSpec(shape, lambda g, where: zeros)] * count,
            out_specs=pl.BlockSpec((1,) + shape, lambda g, where: (where[g],) + zeros),
        ),
        compiler_params=pltpu.CompilerParams(vmem_limit_bytes=VMEM_LIMIT),
        cost_estimate=pl.CostEstimate(
            flops=0, transcendentals=0, bytes_accessed=2 * count * pieces[0].nbytes
        ),
    )(jnp.stack([jnp.asarray(i, jnp.int32) for i in order]), *pieces)


def join(pieces):
    return place(pieces, range(len(pieces))).reshape((-1,) + pieces[0].shape[1:])


def pack_qkv(w_query, w_key, w_value, t_of, n_t):
    rows = w_query.shape[0]
    q, kv = w_query.shape[1] // n_t, w_key.shape[1] // n_t
    n_f = len(t_of)

    def body(where, wq, wk, wv, *outs):
        for d in range(n_f):
            for t in range(n_t):

                @pl.when(where[d] == t)
                def _(d=d, t=t):
                    outs[d][:, :q] = wq[:, t * q : (t + 1) * q]
                    outs[d][:, q : q + kv] = wk[:, t * kv : (t + 1) * kv]
                    outs[d][:, q + kv :] = wv[:, t * kv : (t + 1) * kv]

    block = rows // 4
    return pl.pallas_call(
        body,
        out_shape=[jax.ShapeDtypeStruct((rows, q + 2 * kv), BF16)] * n_f,
        grid_spec=pltpu.PrefetchScalarGridSpec(
            num_scalar_prefetch=1,
            grid=(4,),
            in_specs=[
                pl.BlockSpec((block, w.shape[1]), lambda i, where: (i, 0))
                for w in (w_query, w_key, w_value)
            ],
            out_specs=[pl.BlockSpec((block, q + 2 * kv), lambda i, where: (i, 0))] * n_f,
        ),
        cost_estimate=pl.CostEstimate(
            flops=0, transcendentals=0, bytes_accessed=2 * w_query.nbytes
        ),
    )(jnp.stack(t_of).astype(jnp.int32), w_query, w_key, w_value)


def slice_columns(weight, t_of, size):
    rows, n_f = weight.shape[0], len(t_of)

    def body(where, *refs):
        for d in range(n_f):
            refs[n_f + d][...] = refs[d][...]

    block = rows // 4

    def in_map(d):
        return lambda i, where: (i, where[d])

    return pl.pallas_call(
        body,
        out_shape=[jax.ShapeDtypeStruct((rows, size), weight.dtype)] * n_f,
        grid_spec=pltpu.PrefetchScalarGridSpec(
            num_scalar_prefetch=1,
            grid=(4,),
            in_specs=[pl.BlockSpec((block, size), in_map(d)) for d in range(n_f)],
            out_specs=[pl.BlockSpec((block, size), lambda i, where: (i, 0))] * n_f,
        ),
        cost_estimate=pl.CostEstimate(
            flops=0, transcendentals=0, bytes_accessed=4 * n_f * rows * size
        ),
    )(jnp.stack(t_of).astype(jnp.int32), *[weight] * n_f)


def assemble_blocks(pieces, rows_of, core):
    n_z, n_c = len(pieces), len(pieces[0])
    n_f, rows, columns = pieces[0][0].shape
    flat = [piece for pair in pieces for piece in pair]
    count = len(flat)
    where = jnp.stack([jnp.asarray(i, jnp.int32) for i in rows_of] + [core.astype(jnp.int32)])

    def body(where, *refs):
        out = refs[count]
        for s in range(n_z):
            for own in range(n_c):

                @pl.when((pl.program_id(0) == s) & (where[n_z] == own))
                def _(s=s, own=own):
                    for e in range(n_c):
                        for i in range(n_f):
                            t = i * n_c + (own ^ e)
                            out[:, t * columns : (t + 1) * columns] = refs[s * n_c + e][i].astype(F32)

    return pl.pallas_call(
        body,
        out_shape=jax.ShapeDtypeStruct((n_z * rows, n_f * n_c * columns), F32),
        grid_spec=pltpu.PrefetchScalarGridSpec(
            num_scalar_prefetch=1,
            grid=(n_z,),
            in_specs=[pl.BlockSpec((n_f, rows, columns), lambda g, where: (0, 0, 0))] * count,
            out_specs=pl.BlockSpec((rows, n_f * n_c * columns), lambda g, where: (where[g], 0)),
        ),
        compiler_params=pltpu.CompilerParams(vmem_limit_bytes=VMEM_LIMIT),
        cost_estimate=pl.CostEstimate(
            flops=0, transcendentals=0, bytes_accessed=3 * count * flat[0].nbytes
        ),
    )(where, *flat)


def assemble_rows(pieces, rows_of):
    count = len(pieces)
    rows, columns = pieces[0].shape
    where = jnp.stack([jnp.asarray(i, jnp.int32) for i in rows_of])

    def body(where, *refs):
        for p in range(count):

            @pl.when(pl.program_id(0) == p)
            def _(p=p):
                refs[count][...] = refs[p][...].astype(F32)

    return pl.pallas_call(
        body,
        out_shape=jax.ShapeDtypeStruct((count * rows, columns), F32),
        grid_spec=pltpu.PrefetchScalarGridSpec(
            num_scalar_prefetch=1,
            grid=(count,),
            in_specs=[pl.BlockSpec((rows, columns), lambda g, where: (0, 0))] * count,
            out_specs=pl.BlockSpec((rows, columns), lambda g, where: (where[g], 0)),
        ),
        compiler_params=pltpu.CompilerParams(vmem_limit_bytes=VMEM_LIMIT),
        cost_estimate=pl.CostEstimate(
            flops=0, transcendentals=0, bytes_accessed=3 * count * pieces[0].nbytes
        ),
    )(where, *pieces)


def assemble_qkv(pieces, rows_of, core, n_c, q, kv):
    n_z = len(pieces)
    n_f, rows, columns = pieces[0][0].shape
    flat = [piece for pair in pieces for piece in pair]
    n_t = n_f * n_c
    where = jnp.stack([jnp.asarray(i, jnp.int32) for i in rows_of] + [core.astype(jnp.int32)])

    def body(where, *refs):
        ins, (out_q, out_k, out_v) = refs[: len(flat)], refs[len(flat) :]
        for s in range(n_z):
            for own in range(n_c):

                @pl.when((pl.program_id(0) == s) & (where[n_z] == own))
                def _(s=s, own=own):
                    for e in range(n_c):
                        block = ins[s * n_c + e]
                        for i in range(n_f):
                            t = i * n_c + (own ^ e)
                            part = block[i].astype(F32)
                            out_q[:, t * q : (t + 1) * q] = part[:, :q]
                            out_k[:, t * kv : (t + 1) * kv] = part[:, q : q + kv]
                            out_v[:, t * kv : (t + 1) * kv] = part[:, q + kv :]

    return pl.pallas_call(
        body,
        out_shape=[
            jax.ShapeDtypeStruct((n_z * rows, n_t * w), F32) for w in (q, kv, kv)
        ],
        grid_spec=pltpu.PrefetchScalarGridSpec(
            num_scalar_prefetch=1,
            grid=(n_z,),
            in_specs=[pl.BlockSpec((n_f, rows, columns), lambda g, where: (0, 0, 0))] * len(flat),
            out_specs=[
                pl.BlockSpec((rows, n_t * w), lambda g, where: (where[g], 0)) for w in (q, kv, kv)
            ],
        ),
        compiler_params=pltpu.CompilerParams(vmem_limit_bytes=VMEM_LIMIT),
        cost_estimate=pl.CostEstimate(
            flops=0, transcendentals=0, bytes_accessed=3 * len(flat) * flat[0].nbytes
        ),
    )(where, *flat)


def swap(value, axis, offset):
    size = lax.axis_size(axis)
    return lax.ppermute(value, axis, [(i, i ^ offset) for i in range(size)])


def gather_plane(own):
    n_f, n_c = lax.axis_size("f"), lax.axis_size("core")
    rows = own.shape[0]
    if n_f == 4 and rows % 32 == 0:
        half = rows // 2
        from_x = swap(own, "f", 1)
        from_y = swap(own, "f", 2)
        far_low = swap(from_x[:half], "f", 2)
        far_high = swap(from_y[half:], "f", 1)
        mine = [own, from_x, from_y, jnp.concatenate([far_low, far_high], axis=0)]
    else:
        mine = [own] + [swap(own, "f", d) for d in range(1, n_f)]
    blocks = []
    for part in mine:
        blocks.append(part)
        if n_c == 2:
            blocks.append(swap(part, "core", 1))
    return blocks


def scatter_plane(parts):
    n_f, n_c = lax.axis_size("f"), lax.axis_size("core")
    if n_c == 2:
        sums = []
        for d in range(n_f):
            sums.append(parts[d, 0] + swap(parts[d, 1].astype(BF16), "core", 1).astype(F32))
    else:
        sums = [parts[d, 0] for d in range(n_f)]
    rows = sums[0].shape[0]
    if n_f == 4 and rows % 32 == 0:
        half = rows // 2
        far = sums[3].astype(BF16)
        via_x = swap(far[:half], "f", 1).astype(F32)
        via_y = swap(far[half:], "f", 2).astype(F32)
        x_low = swap(sums[1][:half].astype(BF16), "f", 1)
        y_high = swap(sums[2][half:].astype(BF16), "f", 2)
        x_high = swap((sums[1][half:] + via_y).astype(BF16), "f", 1)
        y_low = swap((sums[2][:half] + via_x).astype(BF16), "f", 2)
        low = sums[0][:half] + x_low.astype(F32) + y_low.astype(F32)
        high = sums[0][half:] + x_high.astype(F32) + y_high.astype(F32)
        return jnp.concatenate([low, high], axis=0)
    total = sums[0]
    for d in range(1, n_f):
        total = total + swap(sums[d].astype(BF16), "f", d).astype(F32)
    return total


def pick(parts, index):
    return lax.dynamic_index_in_dim(parts, index, 0, keepdims=False)


def sum_along_z(parts, z_axis=0):
    n_z, z = lax.axis_size("z"), lax.axis_index("z")

    def chunk(k):
        return lax.dynamic_index_in_dim(
            parts, jnp.clip(k, 0, n_z - 1), z_axis, keepdims=False
        )

    up = down = None
    for step in range(1, n_z):
        send_up = chunk(z + n_z - step)
        send_down = chunk(z - n_z + step)
        if up is not None:
            send_up = (send_up.astype(F32) + up.astype(F32)).astype(BF16)
            send_down = (send_down.astype(F32) + down.astype(F32)).astype(BF16)
        up = lax.ppermute(send_up, "z", [(i, i + 1) for i in range(step)])
        down = lax.ppermute(send_down, "z", [(i, i - 1) for i in range(n_z - step, n_z)])
    total = chunk(z).astype(F32)
    if up is not None:
        total = total + up.astype(F32) + down.astype(F32)
    return total.astype(BF16)


def spread_along_z(own):
    n_z, z = lax.axis_size("z"), lax.axis_index("z")
    ups, downs = [own], [own]
    for step in range(1, n_z):
        ups.append(lax.ppermute(ups[-1], "z", [(i, i + 1) for i in range(step - 1, n_z - 1)]))
        downs.append(lax.ppermute(downs[-1], "z", [(i, i - 1) for i in range(1, n_z - step + 1)]))
    return [own] + [jnp.where(z >= s, ups[s], downs[n_z - s]) for s in range(1, n_z)]


def turn_along_z(own):
    n_z = lax.axis_size("z")
    return [own] + [
        lax.ppermute(own, "z", [(i, (i + s) % n_z) for i in range(n_z)]) for s in range(1, n_z)
    ]


def rms_parts(values):
    inverse = lax.rsqrt(jnp.mean(values * values, axis=-1, keepdims=True) + EPS)
    return values * inverse, inverse


def rms_backward(grad_normed, unit_rows, inverse, norm_gain):
    scaled = grad_normed * norm_gain
    grad_rows = inverse * (
        scaled - unit_rows * jnp.mean(scaled * unit_rows, axis=-1, keepdims=True)
    )
    return jnp.sum(grad_normed * unit_rows, axis=0), grad_rows


def rotate(values, cosine, sine):
    half = values.shape[1] // 2
    a, b = values[:, :half], values[:, half:]
    return jnp.concatenate([a * cosine - b * sine, b * cosine + a * sine], axis=1)


def rotate_back(grads, cosine, sine):
    half = grads.shape[1] // 2
    a, b = grads[:, :half], grads[:, half:]
    return jnp.concatenate([a * cosine + b * sine, b * cosine - a * sine], axis=1)


def dot(a, b, contract):
    return lax.dot_general(a, b, (contract, ((), ())), preferred_element_type=F32)


def stack_at(pieces, order):
    result = jnp.stack(pieces)
    for piece, index in zip(pieces, order, strict=True):
        result = lax.dynamic_update_index_in_dim(result, piece, index, 0)
    return result


def per_device(
    tokens, doc_starts, gain_one, w_query, w_key, w_value, w_out, gain_two, w_gate, w_up, w_down,
    cotangent,
):
    n_z, n_c, n_f = lax.axis_size("z"), lax.axis_size("core"), lax.axis_size("f")
    z, c, f = lax.axis_index("z"), lax.axis_index("core"), lax.axis_index("f")
    n_t = n_f * n_c
    block_len, width = tokens.shape[3], tokens.shape[4]
    rows = 2 * block_len
    plane = n_t * rows
    shard = width // n_f
    q_width = w_query.shape[1] // n_t
    kv_width = w_key.shape[1] // n_t
    hidden = w_gate.shape[1] // n_t
    qkv_width = q_width + 2 * kv_width
    heads = q_width // HEAD_SIZE

    own_x = tokens.reshape(rows, width)
    own_dy = cotangent.reshape(rows, width)
    t_of = [(f ^ d) * n_c + c for d in range(n_f)]

    qkv_parts = pack_qkv(w_query, w_key, w_value, t_of, n_t)
    qkv_parts = [qkv_parts[0]] + [swap(qkv_parts[d], "f", d) for d in range(1, n_f)]
    f_order = [f ^ d for d in range(n_f)]
    w_qkv = place(qkv_parts, f_order).reshape(width, qkv_width)

    gains = jnp.stack([gain_one, gain_two])
    gains = stack_at([gains] + [swap(gains, "f", d) for d in range(1, n_f)], f_order)
    gains = jnp.transpose(gains, (1, 0, 2)).reshape(2, width).astype(F32)
    gain_one_full, gain_two_full = gains[0], gains[1]

    x_all = join(gather_plane(own_x))
    starts_all = jnp.concatenate(gather_plane(doc_starts.reshape(1, rows)), axis=0)
    starts_all = starts_all.reshape(n_f, n_c * rows)

    def ctx_positions(z_index, core_offset):
        device = z_index * n_c + (c ^ core_offset)
        within = jnp.arange(rows, dtype=jnp.int32)
        return jnp.where(
            within < block_len,
            device * block_len + within,
            (2 * n_z * n_c - 1 - device) * block_len + within - block_len,
        )

    q_pos = jnp.concatenate([ctx_positions(z, e) for e in range(n_c)])
    k_pos = jnp.concatenate(
        [ctx_positions((z - s) % n_z, e) for s in range(n_z) for e in range(n_c)]
    )
    rel_pos = (q_pos[None, :] - starts_all).astype(F32).reshape(plane)
    inv_freq = THETA ** (-(jnp.arange(HEAD_SIZE // 2, dtype=F32) * 2.0) / HEAD_SIZE)
    angles = inv_freq[:, None] * rel_pos[None, :]
    cosine, sine = jnp.cos(angles), jnp.sin(angles)

    def ffn_slices(weight, *earlier):
        parts = slice_columns(weight, t_of, hidden)
        parts = [parts[0]] + [swap(after(parts[d], *earlier), "f", d) for d in range(1, n_f)]
        return place(parts, f_order).reshape(width, hidden)

    h_one = (rms_parts(x_all.astype(F32))[0] * gain_one_full).astype(BF16)
    qkv = dot(w_qkv, h_one, ((0,), (1,)))
    query = rotate(qkv[:q_width].reshape(heads, HEAD_SIZE, plane), cosine, sine)
    query = (query * HEAD_SIZE ** (-0.5)).astype(BF16)
    key = rotate(qkv[q_width : q_width + kv_width].reshape(1, HEAD_SIZE, plane), cosine, sine)
    key_value = jnp.concatenate([key[0].astype(BF16), qkv[q_width + kv_width :].astype(BF16)], axis=0)

    gate_full = ffn_slices(w_gate, key_value)
    up_full = ffn_slices(w_up, key_value)
    dy_all = join(gather_plane(after(own_dy, key_value)))

    kv_all = jnp.stack(turn_along_z(key_value))
    span = n_c * rows
    kv_all = kv_all.reshape(n_z, 2, HEAD_SIZE, n_f, span)
    kv_all = jnp.transpose(kv_all, (1, 3, 2, 0, 4)).reshape(2, n_f, HEAD_SIZE, n_z * span)
    keys, values = kv_all[0], kv_all[1]
    queries = jnp.transpose(query.reshape(heads, HEAD_SIZE, n_f, span), (2, 0, 1, 3))
    visible = (k_pos[None, None, :] >= starts_all[:, :, None]) & (
        k_pos[None, None, :] <= q_pos[None, :, None]
    )
    visible = visible[:, None]
    scores = jnp.einsum("shcq,sck->shqk", queries, keys, preferred_element_type=F32)
    masked = jnp.where(visible, scores, NEGATIVE_LARGE)
    row_max = jnp.max(masked, axis=-1, keepdims=True)
    terms = jnp.where(visible, jnp.exp(masked - row_max), 0.0)
    probs = terms / jnp.sum(terms, axis=-1, keepdims=True)
    probs_low = probs.astype(BF16)
    attn = jnp.einsum("shqk,sck->shcq", probs_low, values, preferred_element_type=F32)
    attn_low = jnp.transpose(attn.astype(BF16), (1, 2, 0, 3)).reshape(q_width, plane)

    out_rows = lax.dynamic_slice_in_dim(w_out, c * q_width, q_width, 0)
    projected = dot(attn_low, out_rows, ((0,), (0,)))
    residual = own_x.astype(F32)
    middle = residual + scatter_plane(projected.reshape(n_f, n_c, rows, width))
    unit_two, inv_two = rms_parts(middle)
    h_two_own = (unit_two * gain_two_full).astype(BF16)
    h_two = join(gather_plane(h_two_own))

    down_rows = lax.dynamic_slice_in_dim(w_down, c * hidden, hidden, 0)
    gate = dot(h_two, gate_full, ((1,), (0,)))
    up = dot(h_two, up_full, ((1,), (0,)))
    sigmoid = jax.nn.sigmoid(gate)
    silu = gate * sigmoid
    mid = (silu * up).astype(BF16)
    grad_down = dot(mid, dy_all, ((0,), (0,))).astype(BF16)
    grad_mid = dot(dy_all, down_rows, ((1,), (1,)))
    grad_g = (grad_mid * up * sigmoid * (1.0 + gate * (1.0 - sigmoid))).astype(BF16)
    grad_u = (grad_mid * silu).astype(BF16)
    grad_h_two = dot(grad_g, gate_full, ((1,), (1,))) + dot(grad_u, up_full, ((1,), (1,)))
    grad_gate = dot(h_two, grad_g, ((0,), (0,))).astype(BF16)
    grad_up = dot(h_two, grad_u, ((0,), (0,))).astype(BF16)
    grad_h_two = scatter_plane(grad_h_two.reshape(n_f, n_c, rows, width))
    mixed = middle + scatter_plane(
        dot(mid, down_rows, ((1,), (0,))).reshape(n_f, n_c, rows, width)
    )
    grad_gain_two, grad_norm = rms_backward(grad_h_two, unit_two, inv_two, gain_two_full)
    grad_middle = own_dy.astype(F32) + grad_norm

    grad_branch = join(gather_plane(grad_middle.astype(BF16)))
    grad_attn = dot(out_rows, grad_branch, ((1,), (1,))).astype(BF16)
    grad_out = dot(attn_low, grad_branch, ((1,), (0,))).astype(BF16)
    grad_attn = jnp.transpose(grad_attn.reshape(heads, HEAD_SIZE, n_f, span), (2, 0, 1, 3))
    delta = jnp.sum(grad_attn.astype(F32) * attn, axis=2)
    grad_values = jnp.einsum("shqk,shcq->sck", probs_low, grad_attn, preferred_element_type=F32)
    grad_probs = jnp.einsum("shcq,sck->shqk", grad_attn, values, preferred_element_type=F32)
    grad_scores = (probs * (grad_probs - delta[..., None])).astype(BF16)
    grad_query = jnp.einsum("shqk,sck->shcq", grad_scores, keys, preferred_element_type=F32)
    grad_keys = jnp.einsum("shqk,shcq->sck", grad_scores, queries, preferred_element_type=F32)
    grad_kv = jnp.concatenate([grad_keys, grad_values], axis=1)
    grad_kv = grad_kv.reshape(n_f, 2 * HEAD_SIZE, n_z, span)
    grad_kv = jnp.transpose(grad_kv, (2, 1, 0, 3)).reshape(n_z, 2 * HEAD_SIZE, plane)
    kv_total = grad_kv[0]
    for s in range(1, n_z):
        kv_total = kv_total + lax.ppermute(
            grad_kv[s].astype(BF16), "z", [(i, (i - s) % n_z) for i in range(n_z)]
        ).astype(F32)
    grad_query = jnp.transpose(grad_query, (1, 2, 0, 3)).reshape(heads, HEAD_SIZE, plane)
    grad_qkv = jnp.concatenate(
        [
            rotate_back(grad_query * HEAD_SIZE ** (-0.5), cosine, sine).reshape(q_width, plane),
            rotate_back(kv_total[None, :HEAD_SIZE], cosine, sine)[0],
            kv_total[HEAD_SIZE:],
        ],
        axis=0,
    ).astype(BF16)
    grad_h_one = dot(grad_qkv, w_qkv, ((0,), (1,)))
    grad_w_qkv = dot(h_one, grad_qkv, ((0,), (1,))).astype(BF16)
    grad_h_one = scatter_plane(grad_h_one.reshape(n_f, n_c, rows, width))
    unit_one, inv_one = rms_parts(residual)
    grad_gain_one, grad_norm = rms_backward(grad_h_one, unit_one, inv_one, gain_one_full)
    grad_tokens = grad_middle + grad_norm

    z_order = [(z - s) % n_z for s in range(n_z)]

    def both_cores(own):
        pieces = []
        for piece in spread_along_z(own):
            pieces.append([piece] + [swap(piece, "core", e) for e in range(1, n_c)])
        return pieces

    def finish_rows(grad):
        n_rows = grad.shape[0]
        piece_rows = n_rows // n_z
        pieces = both_cores(sum_along_z(grad.reshape(n_z, piece_rows, width)))
        if piece_rows % 16 == 0:
            return assemble_rows(
                [piece for pair in pieces for piece in pair],
                [(c ^ e) * n_z + zi for zi in z_order for e in range(n_c)],
            )
        result = blank((n_c, n_z, piece_rows, width), F32)
        for pair, zi in zip(pieces, z_order, strict=True):
            for e, piece in enumerate(pair):
                result = lax.dynamic_update_slice(
                    result, piece.astype(F32)[None, None], (c ^ e, zi, 0, 0)
                )
        return result.reshape(n_c * n_rows, width)

    def column_pieces(grad):
        columns = grad.shape[1]
        own = sum_along_z(grad.reshape(n_f, n_z, shard // n_z, columns), 1)
        parts = [pick(own, f)]
        for d in range(1, n_f):
            parts.append(swap(pick(own, f ^ d), "f", d))
        return both_cores(place(parts, f_order))

    def finish_columns(pieces, low, high):
        piece_rows = pieces[0][0].shape[1]
        if piece_rows % 16 == 0:
            return assemble_blocks(pieces, z_order, c)
        out = blank((n_z, piece_rows, n_f, n_c, high - low), F32)
        for pair, zi in zip(pieces, z_order, strict=True):
            for e, piece in enumerate(pair):
                update = jnp.transpose(piece[:, :, low:high].astype(F32), (1, 0, 2))
                out = lax.dynamic_update_slice(out, update[None, :, :, None], (zi, 0, 0, c ^ e, 0))
        return out.reshape(shard, n_t * (high - low))

    total_down = finish_rows(grad_down)
    total_gate = finish_columns(column_pieces(grad_gate), 0, hidden)
    total_up = finish_columns(column_pieces(grad_up), 0, hidden)
    total_out = finish_rows(grad_out)
    qkv_pieces = column_pieces(grad_w_qkv)
    if qkv_pieces[0][0].shape[1] % 16 == 0:
        total_query, total_key, total_value = assemble_qkv(
            qkv_pieces, z_order, c, n_c, q_width, kv_width
        )
    else:
        total_query = finish_columns(qkv_pieces, 0, q_width)
        total_key = finish_columns(qkv_pieces, q_width, q_width + kv_width)
        total_value = finish_columns(qkv_pieces, q_width + kv_width, qkv_width)
    gain_grads = lax.psum(jnp.stack([grad_gain_one, grad_gain_two]), ("z", "core", "f"))
    gain_grads = lax.dynamic_slice_in_dim(gain_grads, f * shard, shard, 1)
    return (
        mixed.reshape(tokens.shape),
        grad_tokens.reshape(tokens.shape),
        gain_grads[0],
        total_query,
        total_key,
        total_value,
        total_out,
        gain_grads[1],
        total_gate,
        total_up,
        total_down,
    )


def solution(mesh):
    n_ctx, n_fsdp = mesh.shape["ctx"], mesh.shape["fsdp"]
    n_core = KEY_VALUE_HEADS // n_fsdp
    inner = Mesh(
        np.asarray(mesh.devices).reshape(n_ctx // n_core, n_core, n_fsdp), ("z", "core", "f")
    )
    ctx = ("z", "core")
    return jax.shard_map(
        per_device,
        mesh=inner,
        in_specs=(
            P("f", ctx, None, None, None),
            P("f", ctx, None, None),
            P("f"),
            P("f", None),
            P("f", None),
            P("f", None),
            P("f", None),
            P("f"),
            P("f", None),
            P("f", None),
            P("f", None),
            P("f", ctx, None, None, None),
        ),
        out_specs=(
            P("f", ctx, None, None, None),
            P("f", ctx, None, None, None),
            P("f"),
            P("f", None),
            P("f", None),
            P("f", None),
            P("f", None),
            P("f"),
            P("f", None),
            P("f", None),
            P("f", None),
        ),
        check_vma=False,
    )
```

```python
import jax
import jax.numpy as jnp
import numpy as np
from jax import lax
from jax.experimental import pallas as pl
from jax.experimental.pallas import tpu as pltpu
from jax.sharding import Mesh
from jax.sharding import PartitionSpec as P

QUERY_HEADS = 32
KEY_VALUE_HEADS = 8
HEAD_SIZE = 80

EPS = 1e-05
THETA = 1000000.0
NEGATIVE_LARGE = -1e30

F32 = jnp.float32
BF16 = jnp.bfloat16

ANY = pl.BlockSpec(memory_space=pl.ANY)
PARAMS = pltpu.CompilerParams(vmem_limit_bytes=56 * 1024 * 1024)


class Order:
    def __init__(self):
        self.last = ()

    def pin(self, *arrays):
        return lax.optimization_barrier(arrays + self.last)[: len(arrays)]

    def region(self, function, *arrays):
        results = function(*self.pin(*arrays))
        single = not isinstance(results, (tuple, list))
        self.last = (results,) if single else tuple(results)
        return results


def scalars(*values):
    return jnp.stack([jnp.asarray(v, jnp.int32) for v in values])


def moved(*arrays):
    return pl.CostEstimate(
        flops=0, transcendentals=0, bytes_accessed=2 * sum(a.size * a.dtype.itemsize for a in arrays)
    )


def whole(shape):
    return pl.BlockSpec(shape, lambda *_: (0,) * len(shape))


def blank(shape, dtype):
    return pl.pallas_call(
        lambda out: None, out_shape=jax.ShapeDtypeStruct(shape, dtype), out_specs=ANY
    )()


def swap(value, axis, offset):
    size = lax.axis_size(axis)
    return lax.ppermute(value, axis, [(i, i ^ offset) for i in range(size)])


def pack_qkv(w_query, w_key, w_value, core, n_f, n_c):
    rows = w_query.shape[0]
    n_t = n_f * n_c
    q, kv = w_query.shape[1] // n_t, w_key.shape[1] // n_t

    def body(where, wq, wk, wv, out):
        for c in range(n_c):

            @pl.when(where[0] == c)
            def _(c=c):
                for f in range(n_f):
                    t = f * n_c + c
                    out[f, :, :q] = wq[:, t * q : (t + 1) * q]
                    out[f, :, q : q + kv] = wk[:, t * kv : (t + 1) * kv]
                    out[f, :, q + kv :] = wv[:, t * kv : (t + 1) * kv]

    block = rows // 4
    return pl.pallas_call(
        body,
        out_shape=jax.ShapeDtypeStruct((n_f, rows, q + 2 * kv), BF16),
        grid_spec=pltpu.PrefetchScalarGridSpec(
            num_scalar_prefetch=1,
            grid=(4,),
            in_specs=[
                pl.BlockSpec((block, w.shape[1]), lambda i, where: (i, 0))
                for w in (w_query, w_key, w_value)
            ],
            out_specs=pl.BlockSpec((n_f, block, q + 2 * kv), lambda i, where: (0, i, 0)),
        ),
        compiler_params=PARAMS,
        cost_estimate=moved(w_query),
    )(scalars(core), w_query, w_key, w_value)


def slice_columns(weight, core, n_f, n_c):
    rows, size = weight.shape[0], weight.shape[1] // (n_f * n_c)

    def body(where, source, out):
        out[0] = source[...]

    return pl.pallas_call(
        body,
        out_shape=jax.ShapeDtypeStruct((n_f, rows, size), weight.dtype),
        grid_spec=pltpu.PrefetchScalarGridSpec(
            num_scalar_prefetch=1,
            grid=(n_f,),
            in_specs=[pl.BlockSpec((rows, size), lambda i, where: (0, i * n_c + where[0]))],
            out_specs=pl.BlockSpec((1, rows, size), lambda i, where: (i, 0, 0)),
        ),
        compiler_params=PARAMS,
        cost_estimate=moved(weight),
    )(scalars(core), weight)


EXTRA = 32
DIGIT = 64


def payload(x, starts, gain_one, gain_two):
    rows, width = x.shape

    def body(x, starts, one, two, out):
        out[:rows] = x[...]
        out[rows : rows + EXTRA] = jnp.zeros((EXTRA, width), BF16)
        low = (starts[...] & (DIGIT - 1)).astype(F32)
        high = (starts[...] // DIGIT).astype(F32)
        for row, value in enumerate((low, high, one[...].astype(F32), two[...].astype(F32))):
            out[rows + row : rows + row + 1, : value.shape[1]] = value.astype(BF16)

    return pl.pallas_call(
        body,
        out_shape=jax.ShapeDtypeStruct((rows + EXTRA, width), BF16),
        compiler_params=PARAMS,
        cost_estimate=moved(x),
    )(x, starts, gain_one, gain_two)


def project_first(payloads, gains, w_qkv, z, n_z, n_c, block_len):
    width, columns = w_qkv.shape
    rows = 2 * block_len
    count = payloads.shape[0] // (rows + EXTRA)
    half = HEAD_SIZE // 2
    q_width = columns - 2 * HEAD_SIZE
    inv_freq = THETA ** (-(jnp.arange(half, dtype=F32) * 2.0) / HEAD_SIZE)

    def body(where, block, gain, w, freq, h_out, q_out, kv_out, cos_out, sin_out, st_out):
        x = block[:rows].astype(F32)
        inverse = lax.rsqrt(jnp.mean(x * x, axis=-1, keepdims=True) + EPS)
        h_out[...] = (x * inverse * gain[0:1]).astype(BF16)
        low, high = block[rows : rows + 1, :rows], block[rows + 1 : rows + 2, :rows]
        start = (low.astype(F32) + high.astype(F32) * DIGIT).astype(jnp.int32)
        st_out[0] = start
        device = where[0] * n_c + lax.rem(pl.program_id(0), n_c)
        within = lax.broadcasted_iota(jnp.int32, (1, rows), 1)
        position = jnp.where(
            within < block_len,
            device * block_len + within,
            (2 * n_z * n_c - 1 - device) * block_len + within - block_len,
        )
        angles = freq[...] * (position - start).astype(F32)
        cosine, sine = jnp.cos(angles), jnp.sin(angles)
        cos_out[...] = cosine
        sin_out[...] = sine
        projected = nn(h_out[...], w[...]).T

        def turned(row):
            a, b = projected[row : row + half], projected[row + half : row + HEAD_SIZE]
            return jnp.concatenate([a * cosine - b * sine, b * cosine + a * sine], axis=0)

        for row in range(0, q_width, HEAD_SIZE):
            q_out[row : row + HEAD_SIZE] = (turned(row) * HEAD_SIZE ** (-0.5)).astype(BF16)
        kv_out[:HEAD_SIZE] = turned(q_width).astype(BF16)
        kv_out[HEAD_SIZE:] = projected[q_width + HEAD_SIZE :].astype(BF16)

    tokens = count * rows

    def lanes(size):
        return pl.BlockSpec((size, rows), lambda g, where: (0, g))

    return pl.pallas_call(
        body,
        out_shape=[
            jax.ShapeDtypeStruct((tokens, width), BF16),
            jax.ShapeDtypeStruct((q_width, tokens), BF16),
            jax.ShapeDtypeStruct((2 * HEAD_SIZE, tokens), BF16),
            jax.ShapeDtypeStruct((half, tokens), F32),
            jax.ShapeDtypeStruct((half, tokens), F32),
            jax.ShapeDtypeStruct((count, 1, rows), jnp.int32),
        ],
        grid_spec=pltpu.PrefetchScalarGridSpec(
            num_scalar_prefetch=1,
            grid=(count,),
            in_specs=[
                pl.BlockSpec((rows + EXTRA, width), lambda g, where: (g, 0)),
                whole(gains.shape),
                whole(w_qkv.shape),
                whole((half, 1)),
            ],
            out_specs=[
                pl.BlockSpec((rows, width), lambda g, where: (g, 0)),
                lanes(q_width),
                lanes(2 * HEAD_SIZE),
                lanes(half),
                lanes(half),
                pl.BlockSpec((1, 1, rows), lambda g, where: (g, 0, 0)),
            ],
        ),
        compiler_params=PARAMS,
        cost_estimate=pl.CostEstimate(
            flops=2 * tokens * width * columns,
            transcendentals=tokens * HEAD_SIZE,
            bytes_accessed=4 * tokens * width,
        ),
    )(scalars(z), payloads, gains, w_qkv, inv_freq[:, None])


def tn(a, b):
    return lax.dot_general(a, b, (((0,), (0,)), ((), ())), preferred_element_type=F32)


def nt(a, b):
    return lax.dot_general(a, b, (((1,), (1,)), ((), ())), preferred_element_type=F32)


def nn(a, b):
    return lax.dot_general(a, b, (((1,), (0,)), ((), ())), preferred_element_type=F32)


def visible_rows(k_pos, q_pos, starts):
    return (k_pos >= starts) & (k_pos <= q_pos)


def attention(query, key_values, k_pos, q_pos, starts, n_f):
    width, tokens = query.shape
    heads, span, n_z = width // HEAD_SIZE, tokens // n_f, len(key_values)

    def body(*refs):
        q, kvs = refs[0], refs[1 : 1 + n_z]
        kp, qp, st, out, low, lse = refs[1 + n_z :]
        keys = jnp.concatenate([kv[:HEAD_SIZE] for kv in kvs], axis=1)
        values = jnp.concatenate([kv[HEAD_SIZE:] for kv in kvs], axis=1)
        seen = visible_rows(kp[...], qp[...], st[0])
        for h in range(heads):
            part = slice(h * HEAD_SIZE, (h + 1) * HEAD_SIZE)
            scores = jnp.where(seen, tn(keys, q[part]), NEGATIVE_LARGE)
            top = jnp.max(scores, axis=0, keepdims=True)
            terms = jnp.exp(scores - top)
            total = jnp.sum(terms, axis=0, keepdims=True)
            result = nn(values, terms.astype(BF16)) / total
            out[part] = result
            low[part] = result.astype(BF16)
            lse[0, h : h + 1] = top + jnp.log(total)

    return pl.pallas_call(
        body,
        out_shape=[
            jax.ShapeDtypeStruct((width, tokens), F32),
            jax.ShapeDtypeStruct((width, tokens), BF16),
            jax.ShapeDtypeStruct((n_f, heads, span), F32),
        ],
        grid=(n_f,),
        in_specs=[pl.BlockSpec((width, span), lambda i: (0, i))]
        + [pl.BlockSpec((2 * HEAD_SIZE, span), lambda i: (0, i))] * n_z
        + [
            whole(k_pos.shape),
            whole(q_pos.shape),
            pl.BlockSpec((1, 1, span), lambda i: (i, 0, 0)),
        ],
        out_specs=[
            pl.BlockSpec((width, span), lambda i: (0, i)),
            pl.BlockSpec((width, span), lambda i: (0, i)),
            pl.BlockSpec((1, heads, span), lambda i: (i, 0, 0)),
        ],
        compiler_params=PARAMS,
        cost_estimate=pl.CostEstimate(
            flops=4 * width * tokens * span * n_z,
            transcendentals=heads * tokens * span * n_z,
            bytes_accessed=8 * width * tokens,
        ),
    )(query, *key_values, k_pos, q_pos, starts)


def attention_back(query, key_values, grad, out, lse, k_pos, q_pos, starts, n_f, z_order):
    width, tokens = query.shape
    heads, span, n_z = width // HEAD_SIZE, tokens // n_f, len(key_values)

    def body(where, *refs):
        q, kvs = refs[0], refs[1 : 1 + n_z]
        do, o, l, kp, qp, st, dq = refs[1 + n_z : 8 + n_z]
        dkv = refs[8 + n_z]
        keys = jnp.concatenate([kv[:HEAD_SIZE] for kv in kvs], axis=1)
        values = jnp.concatenate([kv[HEAD_SIZE:] for kv in kvs], axis=1)
        seen = visible_rows(kp[...], qp[...], st[0])
        grad_keys = jnp.zeros((HEAD_SIZE, n_z * span), F32)
        grad_values = jnp.zeros((HEAD_SIZE, n_z * span), F32)
        for h in range(heads):
            part = slice(h * HEAD_SIZE, (h + 1) * HEAD_SIZE)
            scores = jnp.where(seen, tn(keys, q[part]), NEGATIVE_LARGE)
            probs = jnp.exp(scores - l[0, h : h + 1])
            delta = jnp.sum(do[part].astype(F32) * o[part], axis=0, keepdims=True)
            grad_values += nt(do[part], probs.astype(BF16))
            grad_scores = (probs * (tn(values, do[part]) - delta)).astype(BF16)
            dq[part] = nn(keys, grad_scores)
            grad_keys += nt(q[part], grad_scores)
        for s in range(n_z):
            here = slice(s * span, (s + 1) * span)
            dkv[where[s], :HEAD_SIZE] = grad_keys[:, here].astype(BF16)
            dkv[where[s], HEAD_SIZE:] = grad_values[:, here].astype(BF16)

    wide = pl.BlockSpec((width, span), lambda i, where: (0, i))
    narrow = pl.BlockSpec((2 * HEAD_SIZE, span), lambda i, where: (0, i))
    return pl.pallas_call(
        body,
        out_shape=[
            jax.ShapeDtypeStruct((width, tokens), F32),
            jax.ShapeDtypeStruct((n_z, 2 * HEAD_SIZE, tokens), BF16),
        ],
        grid_spec=pltpu.PrefetchScalarGridSpec(
            num_scalar_prefetch=1,
            grid=(n_f,),
            in_specs=[wide]
            + [narrow] * n_z
            + [
                wide,
                wide,
                pl.BlockSpec((1, heads, span), lambda i, where: (i, 0, 0)),
                whole(k_pos.shape),
                whole(q_pos.shape),
                pl.BlockSpec((1, 1, span), lambda i, where: (i, 0, 0)),
            ],
            out_specs=[
                wide,
                pl.BlockSpec((n_z, 2 * HEAD_SIZE, span), lambda i, where: (0, 0, i)),
            ],
        ),
        compiler_params=PARAMS,
        cost_estimate=pl.CostEstimate(
            flops=10 * width * tokens * span * n_z,
            transcendentals=heads * tokens * span * n_z,
            bytes_accessed=12 * width * tokens,
        ),
    )(scalars(*z_order), query, *key_values, grad, out, lse, k_pos, q_pos, starts)


def collect(own, ups, downs, z):
    shape = own.shape
    n_z = len(ups) + 1
    zeros = (0,) * len(shape)

    def body(where, *refs):
        out = refs[2 * n_z - 1]
        k = pl.program_id(0)

        @pl.when(k == where[0])
        def _():
            out[0] = refs[0][...]

        for s in range(1, n_z):

            @pl.when(where[0] - k == s)
            def _(s=s):
                out[0] = refs[s][...]

            @pl.when(k - where[0] == s)
            def _(s=s):
                out[0] = refs[n_z - 1 + s][...]

    return pl.pallas_call(
        body,
        out_shape=jax.ShapeDtypeStruct((n_z,) + shape, own.dtype),
        grid_spec=pltpu.PrefetchScalarGridSpec(
            num_scalar_prefetch=1,
            grid=(n_z,),
            in_specs=[whole(shape)] * (2 * n_z - 1),
            out_specs=pl.BlockSpec((1,) + shape, lambda g, where: (g,) + zeros),
        ),
        compiler_params=PARAMS,
        cost_estimate=moved(*[own] * n_z),
    )(scalars(z), own, *ups, *downs)


def assemble(cores, core, splits):
    n_c = len(cores)
    n_z, n_f, rows, columns = cores[0].shape
    n_t = n_f * n_c

    def body(where, *refs):
        outs = refs[n_c:]
        for own in range(n_c):

            @pl.when(where[0] == own)
            def _(own=own):
                for e in range(n_c):
                    for i in range(n_f):
                        t = i * n_c + (own ^ e)
                        part = refs[e][0, i].astype(F32)
                        for out, (low, high) in zip(outs, splits, strict=True):
                            size = high - low
                            out[:, t * size : (t + 1) * size] = part[:, low:high]

    return pl.pallas_call(
        body,
        out_shape=[
            jax.ShapeDtypeStruct((n_z * rows, n_t * (high - low)), F32) for low, high in splits
        ],
        grid_spec=pltpu.PrefetchScalarGridSpec(
            num_scalar_prefetch=1,
            grid=(n_z,),
            in_specs=[
                pl.BlockSpec((1, n_f, rows, columns), lambda g, where: (g, 0, 0, 0))
                for _ in cores
            ],
            out_specs=[
                pl.BlockSpec((rows, n_t * (high - low)), lambda g, where: (g, 0))
                for low, high in splits
            ],
        ),
        compiler_params=PARAMS,
        cost_estimate=moved(*cores),
    )(scalars(core), *cores)


def assemble_rows(cores, core):
    n_c = len(cores)
    n_z, rows, columns = cores[0].shape

    def body(where, *refs):
        for e in range(n_c):

            @pl.when(pl.program_id(0) == e)
            def _(e=e):
                refs[n_c][...] = refs[e][0].astype(F32)

    def in_map(e):
        return lambda g, k, where: (jnp.clip(k + (g - e) * n_z, 0, n_z - 1), 0, 0)

    return pl.pallas_call(
        body,
        out_shape=jax.ShapeDtypeStruct((n_c * n_z * rows, columns), F32),
        grid_spec=pltpu.PrefetchScalarGridSpec(
            num_scalar_prefetch=1,
            grid=(n_c, n_z),
            in_specs=[pl.BlockSpec((1, rows, columns), in_map(e)) for e in range(n_c)],
            out_specs=pl.BlockSpec(
                (rows, columns), lambda g, k, where: ((where[0] ^ g) * n_z + k, 0)
            ),
        ),
        compiler_params=PARAMS,
        cost_estimate=moved(*cores),
    )(scalars(core), *cores)


def turn_along_z(own):
    n_z = lax.axis_size("z")
    return [own] + [
        lax.ppermute(own, "z", [(i, (i + s) % n_z) for i in range(n_z)]) for s in range(1, n_z)
    ]


def after(value, *earlier):
    return lax.optimization_barrier((value,) + earlier)[0]


class ZSum:
    def __init__(self, parts, z_axis, between=None):
        self.parts, self.z_axis, self.between = parts, z_axis, between
        self.n_z, self.z = lax.axis_size("z"), lax.axis_index("z")
        self.up = self.down = None

    def chunk(self, k):
        k = jnp.clip(k, 0, self.n_z - 1)
        return lax.dynamic_index_in_dim(self.parts, k, self.z_axis, keepdims=False)

    def add(self, step, *earlier):
        n_z = self.n_z
        up, down = self.chunk(self.z + n_z - step), self.chunk(self.z - n_z + step)
        if self.up is not None:
            up = (up.astype(F32) + self.up.astype(F32)).astype(BF16)
            down = (down.astype(F32) + self.down.astype(F32)).astype(BF16)
        if earlier:
            up, down = after(up, *earlier), after(down, *earlier)
        self.up = lax.ppermute(up, "z", [(i, i + 1) for i in range(step)])
        self.down = lax.ppermute(down, "z", [(i, i - 1) for i in range(n_z - step, n_z)])

    def close(self):
        total = self.chunk(self.z).astype(F32)
        total = (total + self.up.astype(F32) + self.down.astype(F32)).astype(BF16)
        self.own = total if self.between is None else self.between(total)
        self.ups, self.downs = [self.own], [self.own]

    def spread(self, step, *earlier):
        n_z = self.n_z
        up, down = self.ups[-1], self.downs[-1]
        if earlier:
            up, down = after(up, *earlier), after(down, *earlier)
        self.ups.append(lax.ppermute(up, "z", [(i, i + 1) for i in range(step - 1, n_z - 1)]))
        self.downs.append(lax.ppermute(down, "z", [(i, i - 1) for i in range(1, n_z - step + 1)]))

    def result(self):
        mine = collect(self.own, self.ups[1:], self.downs[1:], self.z)
        return [mine] + [swap(mine, "core", e) for e in range(1, lax.axis_size("core"))]


def run_sums(sums, waits):
    previous, slot = None, 0

    def due():
        return tuple(waits[slot]()) if slot in waits else ()

    for one in sums:
        n_z = one.n_z
        for step in range(1, n_z):
            earlier = due()
            if previous is not None:
                earlier += (previous.ups[step], previous.downs[step])
            one.add(step, *earlier)
            if previous is not None and step + 1 < n_z:
                previous.spread(step + 1)
            slot += 1
        one.close()
        one.spread(1, *due())
        slot += 1
        previous = one
    for step in range(2, previous.n_z):
        previous.spread(step, *due())
        slot += 1


def rms_parts(values):
    inverse = lax.rsqrt(jnp.mean(values * values, axis=-1, keepdims=True) + EPS)
    return values * inverse, inverse


def rms_backward(grad_normed, unit_rows, inverse, norm_gain):
    scaled = grad_normed * norm_gain
    grad_rows = inverse * (
        scaled - unit_rows * jnp.mean(scaled * unit_rows, axis=-1, keepdims=True)
    )
    return jnp.sum(grad_normed * unit_rows, axis=0), grad_rows


def rotate(values, cosine, sine):
    half = values.shape[1] // 2
    a, b = values[:, :half], values[:, half:]
    return jnp.concatenate([a * cosine - b * sine, b * cosine + a * sine], axis=1)


def rotate_back(grads, cosine, sine):
    half = grads.shape[1] // 2
    a, b = grads[:, :half], grads[:, half:]
    return jnp.concatenate([a * cosine + b * sine, b * cosine - a * sine], axis=1)


def per_device(
    tokens, doc_starts, gain_one, w_query, w_key, w_value, w_out, gain_two, w_gate, w_up, w_down,
    cotangent,
):
    n_z, n_c, n_f = lax.axis_size("z"), lax.axis_size("core"), lax.axis_size("f")
    z, c, f = lax.axis_index("z"), lax.axis_index("core"), lax.axis_index("f")
    n_t = n_f * n_c
    block_len, width = tokens.shape[3], tokens.shape[4]
    rows = 2 * block_len
    plane, span = n_t * rows, n_c * rows
    shard = width // n_f
    q_width = w_query.shape[1] // n_t
    kv_width = w_key.shape[1] // n_t
    hidden = w_gate.shape[1] // n_t
    qkv_width = q_width + 2 * kv_width
    heads = q_width // HEAD_SIZE
    in_plane = ("f", "core")

    own_x = tokens.reshape(rows, width)
    own_dy = cotangent.reshape(rows, width)

    z_order = [(z - s) % n_z for s in range(n_z)]

    order = Order()
    do = order.region

    first = do(
        payload,
        own_x, doc_starts.reshape(1, rows), gain_one.reshape(1, shard), gain_two.reshape(1, shard),
    )
    payloads = lax.all_gather(first, in_plane, axis=0, tiled=True)

    w_qkv = do(lambda *w: pack_qkv(*w, c, n_f, n_c), w_query, w_key, w_value)
    w_qkv = lax.all_to_all(w_qkv, "f", 0, 0)
    gate_parts, up_parts = do(
        lambda *w: [slice_columns(x, c, n_f, n_c) for x in w], w_gate, w_up
    )

    def project(payloads, w_qkv):
        gains = payloads.reshape(n_f, n_c, rows + EXTRA, width)[:, 0, rows + 2 : rows + 4, :shard]
        gains = jnp.transpose(gains, (1, 0, 2)).reshape(2, width).astype(F32)
        w_qkv = w_qkv.reshape(width, qkv_width)
        return (gains, w_qkv) + tuple(
            project_first(payloads, gains, w_qkv, z, n_z, n_c, block_len)
        )

    payloads, w_qkv = order.pin(payloads, w_qkv)
    gate_full = lax.all_to_all(
        lax.optimization_barrier((gate_parts, w_qkv))[0], "f", 0, 0
    )
    gains, w_qkv, h_one, query, key_value, cosine, sine, starts = do(project, payloads, w_qkv)
    gain_one_full, gain_two_full = gains[0], gains[1]
    starts = starts.reshape(n_f, 1, span)
    (early_dy,) = order.pin(own_dy)
    dy_all = lax.all_gather(early_dy, in_plane, axis=0, tiled=True)

    def positions(z_index):
        device = z_index * n_c + jnp.arange(n_c, dtype=jnp.int32)[:, None]
        within = jnp.arange(rows, dtype=jnp.int32)[None, :]
        return jnp.where(
            within < block_len,
            device * block_len + within,
            (2 * n_z * n_c - 1 - device) * block_len + within - block_len,
        ).reshape(span)

    q_pos = positions(z)[None, :]
    k_pos = jnp.concatenate([positions(zi) for zi in z_order])[:, None]

    key_values = turn_along_z(key_value)
    attn, attn_low, lse = do(
        lambda query, *kvs: attention(query, kvs, k_pos, q_pos, starts, n_f), query, *key_values
    )
    def reduce_plane(value):
        return lax.psum_scatter(value, in_plane, scatter_dimension=0, tiled=True)

    residual = own_x.astype(F32)
    def project_out(attn_low, w_out, gate_full):
        rows_of = lax.dynamic_slice_in_dim(w_out, c * q_width, q_width, 0)
        return rows_of, tn(attn_low, rows_of).astype(BF16), gate_full

    out_rows, projected, gate_full = do(project_out, attn_low, w_out, gate_full)
    (up_parts,) = order.pin(up_parts)
    up_full = lax.all_to_all(up_parts, "f", 0, 0).reshape(width, hidden)
    gate_full = gate_full.reshape(width, hidden)

    def after_attention(reduced, up_full):
        middle = residual + reduced.astype(F32)
        unit, inverse = rms_parts(middle)
        return middle, unit, inverse, (unit * gain_two_full).astype(BF16), up_full

    middle, unit_two, inv_two, h_two, up_full = do(
        after_attention, reduce_plane(projected), up_full
    )
    h_two = lax.all_gather(h_two, in_plane, axis=0, tiled=True)

    def forward(h_two, gate_full, up_full):
        gate, up = nn(h_two, gate_full), nn(h_two, up_full)
        return gate, up, (gate * jax.nn.sigmoid(gate) * up).astype(BF16)

    gate, up, mid = do(forward, h_two, gate_full, up_full)
    down_rows = do(lambda w: lax.dynamic_slice_in_dim(w, c * hidden, hidden, 0), w_down)

    def work(dy, down_rows, gate, up):
        sigmoid = jax.nn.sigmoid(gate)
        grad_mid = nt(dy, down_rows)
        grad_g = (grad_mid * up * sigmoid * (1.0 + gate * (1.0 - sigmoid))).astype(BF16)
        return grad_g, (grad_mid * (gate * sigmoid)).astype(BF16)

    grad_g, grad_u = do(work, dy_all, down_rows, gate, up)
    h_two_parts = do(lambda g, u: (nt(g, gate_full) + nt(u, up_full)).astype(BF16), grad_g, grad_u)
    h_two_back = reduce_plane(h_two_parts)

    grad_down = tn(mid, dy_all).astype(BF16)
    grad_gate = tn(h_two, grad_g).astype(BF16)
    grad_up = tn(h_two, grad_u).astype(BF16)
    grad_gain_two, grad_norm = rms_backward(
        h_two_back.astype(F32), unit_two, inv_two, gain_two_full
    )
    grad_middle = own_dy.astype(F32) + grad_norm

    branch_low = grad_middle.astype(BF16)
    grad_branch = lax.all_gather(branch_low, in_plane, axis=0, tiled=True)
    grad_attn = nt(out_rows, grad_branch).astype(BF16)
    grad_out = nn(attn_low, grad_branch).astype(BF16)
    grad_query, grad_kv = attention_back(
        query, key_values, grad_attn, attn, lse, k_pos, q_pos, starts, n_f, z_order
    )
    kv_total = jnp.sum(lax.all_to_all(grad_kv, "z", 0, 0).astype(F32), axis=0)
    grad_query = grad_query.reshape(heads, HEAD_SIZE, plane) * HEAD_SIZE ** (-0.5)
    grad_qkv = jnp.concatenate(
        [
            rotate_back(grad_query, cosine, sine).reshape(q_width, plane),
            rotate_back(kv_total[None, :HEAD_SIZE], cosine, sine)[0],
            kv_total[HEAD_SIZE:],
        ],
        axis=0,
    ).astype(BF16)
    grad_w_qkv = lax.dot_general(
        h_one, grad_qkv, (((0,), (1,)), ((), ())), preferred_element_type=F32
    ).astype(BF16)
    h_one_parts = lax.dot_general(
        grad_qkv, w_qkv, (((0,), (1,)), ((), ())), preferred_element_type=F32
    ).astype(BF16)
    mixed_parts = nn(mid, down_rows).astype(BF16)
    mixed = middle + reduce_plane(after(mixed_parts, grad_branch)).astype(F32)
    grad_h_one = reduce_plane(h_one_parts).astype(F32)
    unit_one, inv_one = rms_parts(residual)
    grad_gain_one, grad_norm = rms_backward(grad_h_one, unit_one, inv_one, gain_one_full)
    grad_tokens = grad_middle + grad_norm
    gains = jnp.stack([grad_gain_one, grad_gain_two])
    for axis, size in (("z", n_z), ("f", n_f), ("core", n_c)):
        for bit in range(size.bit_length() - 1):
            gains = gains + swap(gains, axis, 1 << bit)
    gain_grads = lax.dynamic_slice_in_dim(gains, f * shard, shard, 1)

    def to_shards(grad):
        return lax.all_to_all(grad, "f", 0, 0)

    def by_z(grad, axis):
        shape = grad.shape
        return grad.reshape(shape[:axis] + (n_z, shape[axis] // n_z) + shape[axis + 1 :])

    gate_shards = to_shards(grad_gate.reshape(n_f, shard, hidden))
    up_shards = to_shards(after(grad_up.reshape(n_f, shard, hidden), gate_shards))
    sum_down = ZSum(by_z(grad_down, 0), 0)
    sum_gate = ZSum(by_z(gate_shards, 1), 1)
    sum_up = ZSum(by_z(up_shards, 1), 1)
    sum_out = ZSum(by_z(grad_out, 0), 0)
    sum_qkv = ZSum(by_z(grad_w_qkv.reshape(n_f, shard, qkv_width), 1), 1, to_shards)
    def finish_rows(one):
        cores = one.result()
        piece_rows, columns = cores[0].shape[1:]
        if piece_rows % 8 == 0:
            return assemble_rows(cores, c)
        result = blank((n_c, n_z, piece_rows, columns), F32)
        for e, piece in enumerate(cores):
            result = lax.dynamic_update_index_in_dim(result, piece.astype(F32), c ^ e, 0)
        return result.reshape(-1, columns)

    def finish_columns(one, splits):
        cores = one.result()
        piece_rows = cores[0].shape[2]
        if piece_rows % 8 == 0:
            return assemble(cores, c, splits)
        results = []
        for low, high in splits:
            out = blank((n_z, piece_rows, n_f, n_c, high - low), F32)
            for e, piece in enumerate(cores):
                update = jnp.transpose(piece[..., low:high].astype(F32), (0, 2, 1, 3))
                out = lax.dynamic_update_index_in_dim(out, update, c ^ e, 3)
            results.append(out.reshape(shard, n_t * (high - low)))
        return results

    totals = {}

    def finish(name, function, *args):
        def get():
            if name not in totals:
                made = function(*args)
                totals[name] = made if isinstance(made, (list, tuple)) else [made]
            return totals[name]

        return get

    down_done = finish("down", finish_rows, sum_down)
    gate_done = finish("gate", finish_columns, sum_gate, [(0, hidden)])
    up_done = finish("up", finish_columns, sum_up, [(0, hidden)])
    out_done = finish("out", finish_rows, sum_out)
    splits = [(0, q_width), (q_width, q_width + kv_width), (q_width + kv_width, qkv_width)]
    qkv_done = finish("qkv", finish_columns, sum_qkv, splits)

    def slot(which, step):
        return which * n_z + min(step, n_z - 1)

    run_sums(
        [sum_down, sum_gate, sum_up, sum_out, sum_qkv],
        {
            slot(3, 0): down_done,
            slot(3, 2): gate_done,
            slot(4, 2): lambda: [*up_done(), gain_grads],
            slot(4, 3): out_done,
        },
    )
    total_down, total_gate, total_up, total_out = (
        done()[0] for done in (down_done, gate_done, up_done, out_done)
    )
    total_query, total_key, total_value = qkv_done()
    return (
        mixed.reshape(tokens.shape),
        grad_tokens.reshape(tokens.shape),
        gain_grads[0],
        total_query,
        total_key,
        total_value,
        total_out,
        gain_grads[1],
        total_gate,
        total_up,
        total_down,
    )


def solution(mesh):
    n_ctx, n_fsdp = mesh.shape["ctx"], mesh.shape["fsdp"]
    n_core = KEY_VALUE_HEADS // n_fsdp
    inner = Mesh(
        np.asarray(mesh.devices).reshape(n_ctx // n_core, n_core, n_fsdp), ("z", "core", "f")
    )
    ctx = ("z", "core")
    return jax.shard_map(
        per_device,
        mesh=inner,
        in_specs=(
            P("f", ctx, None, None, None),
            P("f", ctx, None, None),
            P("f"),
            P("f", None),
            P("f", None),
            P("f", None),
            P("f", None),
            P("f"),
            P("f", None),
            P("f", None),
            P("f", None),
            P("f", ctx, None, None, None),
        ),
        out_specs=(
            P("f", ctx, None, None, None),
            P("f", ctx, None, None, None),
            P("f"),
            P("f", None),
            P("f", None),
            P("f", None),
            P("f", None),
            P("f"),
            P("f", None),
            P("f", None),
            P("f", None),
        ),
        check_vma=False,
    )
```

```python
import jax
import jax.numpy as jnp
import numpy as np
from jax import lax
from jax.experimental import pallas as pl
from jax.experimental.layout import Layout, with_layout_constraint
from jax.experimental.pallas import tpu as pltpu
from jax.sharding import Mesh
from jax.sharding import PartitionSpec as P

QUERY_HEADS = 32
KEY_VALUE_HEADS = 8
HEAD_SIZE = 80

EPS = 1e-05
THETA = 1000000.0
NEGATIVE_LARGE = -1e30

F32 = jnp.float32
BF16 = jnp.bfloat16

ANY = pl.BlockSpec(memory_space=pl.ANY)
PARAMS = pltpu.CompilerParams(vmem_limit_bytes=56 * 1024 * 1024)


class Order:
    def __init__(self):
        self.last = ()

    def pin(self, *arrays):
        return lax.optimization_barrier(arrays + self.last)[: len(arrays)]

    def region(self, function, *arrays):
        results = function(*self.pin(*arrays))
        single = not isinstance(results, (tuple, list))
        self.last = (results,) if single else tuple(results)
        return results


def scalars(*values):
    return jnp.stack([jnp.asarray(v, jnp.int32) for v in values])


def moved(*arrays):
    return pl.CostEstimate(
        flops=0, transcendentals=0, bytes_accessed=2 * sum(a.size * a.dtype.itemsize for a in arrays)
    )


def whole(shape):
    return pl.BlockSpec(shape, lambda *_: (0,) * len(shape))


def blank(shape, dtype):
    return pl.pallas_call(
        lambda out: None, out_shape=jax.ShapeDtypeStruct(shape, dtype), out_specs=ANY
    )()


def swap(value, axis, offset):
    size = lax.axis_size(axis)
    return lax.ppermute(value, axis, [(i, i ^ offset) for i in range(size)])


def pack_qkv(w_query, w_key, w_value, core, n_f, n_c):
    rows = w_query.shape[0]
    n_t = n_f * n_c
    q, kv = w_query.shape[1] // n_t, w_key.shape[1] // n_t

    def body(where, wq, wk, wv, out):
        for c in range(n_c):

            @pl.when(where[0] == c)
            def _(c=c):
                for f in range(n_f):
                    t = f * n_c + c
                    out[f, :, :q] = wq[:, t * q : (t + 1) * q]
                    out[f, :, q : q + kv] = wk[:, t * kv : (t + 1) * kv]
                    out[f, :, q + kv :] = wv[:, t * kv : (t + 1) * kv]

    block = rows // 4
    return pl.pallas_call(
        body,
        out_shape=jax.ShapeDtypeStruct((n_f, rows, q + 2 * kv), BF16),
        grid_spec=pltpu.PrefetchScalarGridSpec(
            num_scalar_prefetch=1,
            grid=(4,),
            in_specs=[
                pl.BlockSpec((block, w.shape[1]), lambda i, where: (i, 0))
                for w in (w_query, w_key, w_value)
            ],
            out_specs=pl.BlockSpec((n_f, block, q + 2 * kv), lambda i, where: (0, i, 0)),
        ),
        compiler_params=PARAMS,
        cost_estimate=moved(w_query),
    )(scalars(core), w_query, w_key, w_value)


def slice_columns(weight, core, n_f, n_c):
    rows, size = weight.shape[0], weight.shape[1] // (n_f * n_c)

    def body(where, source, out):
        out[0] = source[...]

    return pl.pallas_call(
        body,
        out_shape=jax.ShapeDtypeStruct((n_f, rows, size), weight.dtype),
        grid_spec=pltpu.PrefetchScalarGridSpec(
            num_scalar_prefetch=1,
            grid=(n_f,),
            in_specs=[pl.BlockSpec((rows, size), lambda i, where: (0, i * n_c + where[0]))],
            out_specs=pl.BlockSpec((1, rows, size), lambda i, where: (i, 0, 0)),
        ),
        compiler_params=PARAMS,
        cost_estimate=moved(weight),
    )(scalars(core), weight)


EXTRA = 32
DIGIT = 64


def payload(x, starts, gain_one, gain_two):
    rows, width = x.shape

    def body(x, starts, one, two, out):
        out[:rows] = x[...]
        out[rows : rows + EXTRA] = jnp.zeros((EXTRA, width), BF16)
        low = (starts[...] & (DIGIT - 1)).astype(F32)
        high = (starts[...] // DIGIT).astype(F32)
        for row, value in enumerate((low, high, one[...].astype(F32), two[...].astype(F32))):
            out[rows + row : rows + row + 1, : value.shape[1]] = value.astype(BF16)

    return pl.pallas_call(
        body,
        out_shape=jax.ShapeDtypeStruct((rows + EXTRA, width), BF16),
        compiler_params=PARAMS,
        cost_estimate=moved(x),
    )(x, starts, gain_one, gain_two)


def project_first(payloads, gains, w_qkv, z, n_z, n_c, block_len):
    width, columns = w_qkv.shape
    rows = 2 * block_len
    count = payloads.shape[0] // (rows + EXTRA)
    half = HEAD_SIZE // 2
    q_width = columns - 2 * HEAD_SIZE
    inv_freq = THETA ** (-(jnp.arange(half, dtype=F32) * 2.0) / HEAD_SIZE)

    def body(where, block, gain, w, freq, h_out, q_out, kv_out, cos_out, sin_out, st_out):
        x = block[:rows].astype(F32)
        inverse = lax.rsqrt(jnp.mean(x * x, axis=-1, keepdims=True) + EPS)
        h_out[...] = (x * inverse * gain[0:1]).astype(BF16)
        low, high = block[rows : rows + 1, :rows], block[rows + 1 : rows + 2, :rows]
        start = (low.astype(F32) + high.astype(F32) * DIGIT).astype(jnp.int32)
        st_out[0] = start
        device = where[0] * n_c + lax.rem(pl.program_id(0), n_c)
        within = lax.broadcasted_iota(jnp.int32, (1, rows), 1)
        position = jnp.where(
            within < block_len,
            device * block_len + within,
            (2 * n_z * n_c - 1 - device) * block_len + within - block_len,
        )
        angles = freq[...] * (position - start).astype(F32)
        cosine, sine = jnp.cos(angles), jnp.sin(angles)
        cos_out[...] = cosine
        sin_out[...] = sine
        projected = nn(h_out[...], w[...]).T

        def turned(row):
            a, b = projected[row : row + half], projected[row + half : row + HEAD_SIZE]
            return jnp.concatenate([a * cosine - b * sine, b * cosine + a * sine], axis=0)

        for row in range(0, q_width, HEAD_SIZE):
            q_out[row : row + HEAD_SIZE] = (turned(row) * HEAD_SIZE ** (-0.5)).astype(BF16)
        kv_out[:HEAD_SIZE] = turned(q_width).astype(BF16)
        kv_out[HEAD_SIZE:] = projected[q_width + HEAD_SIZE :].astype(BF16)

    tokens = count * rows

    def lanes(size):
        return pl.BlockSpec((size, rows), lambda g, where: (0, g))

    return pl.pallas_call(
        body,
        out_shape=[
            jax.ShapeDtypeStruct((tokens, width), BF16),
            jax.ShapeDtypeStruct((q_width, tokens), BF16),
            jax.ShapeDtypeStruct((2 * HEAD_SIZE, tokens), BF16),
            jax.ShapeDtypeStruct((half, tokens), F32),
            jax.ShapeDtypeStruct((half, tokens), F32),
            jax.ShapeDtypeStruct((count, 1, rows), jnp.int32),
        ],
        grid_spec=pltpu.PrefetchScalarGridSpec(
            num_scalar_prefetch=1,
            grid=(count,),
            in_specs=[
                pl.BlockSpec((rows + EXTRA, width), lambda g, where: (g, 0)),
                whole(gains.shape),
                whole(w_qkv.shape),
                whole((half, 1)),
            ],
            out_specs=[
                pl.BlockSpec((rows, width), lambda g, where: (g, 0)),
                lanes(q_width),
                lanes(2 * HEAD_SIZE),
                lanes(half),
                lanes(half),
                pl.BlockSpec((1, 1, rows), lambda g, where: (g, 0, 0)),
            ],
        ),
        compiler_params=PARAMS,
        cost_estimate=pl.CostEstimate(
            flops=2 * tokens * width * columns,
            transcendentals=tokens * HEAD_SIZE,
            bytes_accessed=4 * tokens * width,
        ),
    )(scalars(z), payloads, gains, w_qkv, inv_freq[:, None])


def tn(a, b):
    return lax.dot_general(a, b, (((0,), (0,)), ((), ())), preferred_element_type=F32)


def nt(a, b):
    return lax.dot_general(a, b, (((1,), (1,)), ((), ())), preferred_element_type=F32)


def nn(a, b):
    return lax.dot_general(a, b, (((1,), (0,)), ((), ())), preferred_element_type=F32)


def visible_rows(k_pos, q_pos, starts):
    return (k_pos >= starts) & (k_pos <= q_pos)


def attention(query, key_values, k_pos, q_pos, starts, n_f):
    width, tokens = query.shape
    heads, span, n_z = width // HEAD_SIZE, tokens // n_f, len(key_values)

    def body(*refs):
        q, kvs = refs[0], refs[1 : 1 + n_z]
        kp, qp, st, out, low, lse = refs[1 + n_z :]
        keys = jnp.concatenate([kv[:HEAD_SIZE] for kv in kvs], axis=1)
        values = jnp.concatenate([kv[HEAD_SIZE:] for kv in kvs], axis=1)
        seen = visible_rows(kp[...], qp[...], st[0])
        for h in range(heads):
            part = slice(h * HEAD_SIZE, (h + 1) * HEAD_SIZE)
            scores = jnp.where(seen, tn(keys, q[part]), NEGATIVE_LARGE)
            top = jnp.max(scores, axis=0, keepdims=True)
            terms = jnp.exp(scores - top)
            total = jnp.sum(terms, axis=0, keepdims=True)
            result = nn(values, terms.astype(BF16)) / total
            out[part] = result
            low[part] = result.astype(BF16)
            lse[0, h : h + 1] = top + jnp.log(total)

    return pl.pallas_call(
        body,
        out_shape=[
            jax.ShapeDtypeStruct((width, tokens), F32),
            jax.ShapeDtypeStruct((width, tokens), BF16),
            jax.ShapeDtypeStruct((n_f, heads, span), F32),
        ],
        grid=(n_f,),
        in_specs=[pl.BlockSpec((width, span), lambda i: (0, i))]
        + [pl.BlockSpec((2 * HEAD_SIZE, span), lambda i: (0, i))] * n_z
        + [
            whole(k_pos.shape),
            whole(q_pos.shape),
            pl.BlockSpec((1, 1, span), lambda i: (i, 0, 0)),
        ],
        out_specs=[
            pl.BlockSpec((width, span), lambda i: (0, i)),
            pl.BlockSpec((width, span), lambda i: (0, i)),
            pl.BlockSpec((1, heads, span), lambda i: (i, 0, 0)),
        ],
        compiler_params=PARAMS,
        cost_estimate=pl.CostEstimate(
            flops=4 * width * tokens * span * n_z,
            transcendentals=heads * tokens * span * n_z,
            bytes_accessed=8 * width * tokens,
        ),
    )(query, *key_values, k_pos, q_pos, starts)


def attention_back(query, key_values, grad, out, lse, k_pos, q_pos, starts, n_f, z_order):
    width, tokens = query.shape
    heads, span, n_z = width // HEAD_SIZE, tokens // n_f, len(key_values)

    def body(where, *refs):
        q, kvs = refs[0], refs[1 : 1 + n_z]
        do, o, l, kp, qp, st, dq = refs[1 + n_z : 8 + n_z]
        dkv = refs[8 + n_z]
        keys = jnp.concatenate([kv[:HEAD_SIZE] for kv in kvs], axis=1)
        values = jnp.concatenate([kv[HEAD_SIZE:] for kv in kvs], axis=1)
        seen = visible_rows(kp[...], qp[...], st[0])
        grad_keys = jnp.zeros((HEAD_SIZE, n_z * span), F32)
        grad_values = jnp.zeros((HEAD_SIZE, n_z * span), F32)
        for h in range(heads):
            part = slice(h * HEAD_SIZE, (h + 1) * HEAD_SIZE)
            scores = jnp.where(seen, tn(keys, q[part]), NEGATIVE_LARGE)
            probs = jnp.exp(scores - l[0, h : h + 1])
            delta = jnp.sum(do[part].astype(F32) * o[part], axis=0, keepdims=True)
            grad_values += nt(do[part], probs.astype(BF16))
            grad_scores = (probs * (tn(values, do[part]) - delta)).astype(BF16)
            dq[part] = nn(keys, grad_scores)
            grad_keys += nt(q[part], grad_scores)
        for s in range(n_z):
            here = slice(s * span, (s + 1) * span)
            dkv[where[s], :HEAD_SIZE] = grad_keys[:, here].astype(BF16)
            dkv[where[s], HEAD_SIZE:] = grad_values[:, here].astype(BF16)

    wide = pl.BlockSpec((width, span), lambda i, where: (0, i))
    narrow = pl.BlockSpec((2 * HEAD_SIZE, span), lambda i, where: (0, i))
    return pl.pallas_call(
        body,
        out_shape=[
            jax.ShapeDtypeStruct((width, tokens), F32),
            jax.ShapeDtypeStruct((n_z, 2 * HEAD_SIZE, tokens), BF16),
        ],
        grid_spec=pltpu.PrefetchScalarGridSpec(
            num_scalar_prefetch=1,
            grid=(n_f,),
            in_specs=[wide]
            + [narrow] * n_z
            + [
                wide,
                wide,
                pl.BlockSpec((1, heads, span), lambda i, where: (i, 0, 0)),
                whole(k_pos.shape),
                whole(q_pos.shape),
                pl.BlockSpec((1, 1, span), lambda i, where: (i, 0, 0)),
            ],
            out_specs=[
                wide,
                pl.BlockSpec((n_z, 2 * HEAD_SIZE, span), lambda i, where: (0, 0, i)),
            ],
        ),
        compiler_params=PARAMS,
        cost_estimate=pl.CostEstimate(
            flops=10 * width * tokens * span * n_z,
            transcendentals=heads * tokens * span * n_z,
            bytes_accessed=12 * width * tokens,
        ),
    )(scalars(*z_order), query, *key_values, grad, out, lse, k_pos, q_pos, starts)


def collect(own, ups, downs, z):
    shape = own.shape
    n_z = len(ups) + 1
    zeros = (0,) * len(shape)

    def body(where, *refs):
        out = refs[2 * n_z - 1]
        k = pl.program_id(0)

        @pl.when(k == where[0])
        def _():
            out[0] = refs[0][...]

        for s in range(1, n_z):

            @pl.when(where[0] - k == s)
            def _(s=s):
                out[0] = refs[s][...]

            @pl.when(k - where[0] == s)
            def _(s=s):
                out[0] = refs[n_z - 1 + s][...]

    return pl.pallas_call(
        body,
        out_shape=jax.ShapeDtypeStruct((n_z,) + shape, own.dtype),
        grid_spec=pltpu.PrefetchScalarGridSpec(
            num_scalar_prefetch=1,
            grid=(n_z,),
            in_specs=[whole(shape)] * (2 * n_z - 1),
            out_specs=pl.BlockSpec((1,) + shape, lambda g, where: (g,) + zeros),
        ),
        compiler_params=PARAMS,
        cost_estimate=moved(*[own] * n_z),
    )(scalars(z), own, *ups, *downs)


def assemble(cores, core, splits):
    n_c = len(cores)
    n_z, n_f, rows, columns = cores[0].shape
    n_t = n_f * n_c

    def body(where, *refs):
        outs = refs[n_c:]
        for own in range(n_c):

            @pl.when(where[0] == own)
            def _(own=own):
                for e in range(n_c):
                    for i in range(n_f):
                        t = i * n_c + (own ^ e)
                        part = refs[e][0, i].astype(F32)
                        for out, (low, high) in zip(outs, splits, strict=True):
                            size = high - low
                            out[:, t * size : (t + 1) * size] = part[:, low:high]

    return pl.pallas_call(
        body,
        out_shape=[
            jax.ShapeDtypeStruct((n_z * rows, n_t * (high - low)), F32) for low, high in splits
        ],
        grid_spec=pltpu.PrefetchScalarGridSpec(
            num_scalar_prefetch=1,
            grid=(n_z,),
            in_specs=[
                pl.BlockSpec((1, n_f, rows, columns), lambda g, where: (g, 0, 0, 0))
                for _ in cores
            ],
            out_specs=[
                pl.BlockSpec((rows, n_t * (high - low)), lambda g, where: (g, 0))
                for low, high in splits
            ],
        ),
        compiler_params=PARAMS,
        cost_estimate=moved(*cores),
    )(scalars(core), *cores)


def assemble_rows(cores, core):
    n_c = len(cores)
    n_z, rows, columns = cores[0].shape

    def body(where, *refs):
        for e in range(n_c):

            @pl.when(pl.program_id(0) == e)
            def _(e=e):
                refs[n_c][...] = refs[e][0].astype(F32)

    def in_map(e):
        return lambda g, k, where: (jnp.clip(k + (g - e) * n_z, 0, n_z - 1), 0, 0)

    return pl.pallas_call(
        body,
        out_shape=jax.ShapeDtypeStruct((n_c * n_z * rows, columns), F32),
        grid_spec=pltpu.PrefetchScalarGridSpec(
            num_scalar_prefetch=1,
            grid=(n_c, n_z),
            in_specs=[pl.BlockSpec((1, rows, columns), in_map(e)) for e in range(n_c)],
            out_specs=pl.BlockSpec(
                (rows, columns), lambda g, k, where: ((where[0] ^ g) * n_z + k, 0)
            ),
        ),
        compiler_params=PARAMS,
        cost_estimate=moved(*cores),
    )(scalars(core), *cores)


def turn_along_z(own):
    n_z = lax.axis_size("z")
    return [own] + [
        lax.ppermute(own, "z", [(i, (i + s) % n_z) for i in range(n_z)]) for s in range(1, n_z)
    ]


def after(value, *earlier):
    return lax.optimization_barrier((value,) + earlier)[0]


class ZSum:
    def __init__(self, parts, z_axis, between=None):
        self.parts, self.z_axis, self.between = parts, z_axis, between
        self.n_z, self.z = lax.axis_size("z"), lax.axis_index("z")
        self.up = self.down = None

    def chunk(self, k):
        k = jnp.clip(k, 0, self.n_z - 1)
        return lax.dynamic_index_in_dim(self.parts, k, self.z_axis, keepdims=False)

    def add(self, step, *earlier):
        n_z = self.n_z
        up, down = self.chunk(self.z + n_z - step), self.chunk(self.z - n_z + step)
        if self.up is not None:
            up = (up.astype(F32) + self.up.astype(F32)).astype(BF16)
            down = (down.astype(F32) + self.down.astype(F32)).astype(BF16)
        if earlier:
            up, down = after(up, *earlier), after(down, *earlier)
        self.sent = (up, down)
        self.up = lax.ppermute(up, "z", [(i, i + 1) for i in range(step)])
        self.down = lax.ppermute(down, "z", [(i, i - 1) for i in range(n_z - step, n_z)])

    def close(self):
        total = self.chunk(self.z).astype(F32)
        total = (total + self.up.astype(F32) + self.down.astype(F32)).astype(BF16)
        self.own = total if self.between is None else self.between(total)
        self.ups, self.downs = [self.own], [self.own]

    def spread(self, step, *earlier):
        n_z = self.n_z
        up, down = self.ups[-1], self.downs[-1]
        if earlier:
            up, down = after(up, *earlier), after(down, *earlier)
        self.ups.append(lax.ppermute(up, "z", [(i, i + 1) for i in range(step - 1, n_z - 1)]))
        self.downs.append(lax.ppermute(down, "z", [(i, i - 1) for i in range(1, n_z - step + 1)]))

    def result(self):
        mine = collect(self.own, self.ups[1:], self.downs[1:], self.z)
        return [mine] + [swap(mine, "core", e) for e in range(1, lax.axis_size("core"))]


def run_sums(previous, sums, waits):
    slot = previous.n_z

    def due():
        return tuple(waits[slot]()) if slot in waits else ()

    for one in sums:
        n_z = one.n_z
        for step in range(1, n_z):
            one.add(step, *due(), previous.ups[step], previous.downs[step])
            if step + 1 < n_z:
                previous.spread(step + 1)
            slot += 1
        one.close()
        one.spread(1, *due())
        slot += 1
        previous = one
    for step in range(2, previous.n_z):
        previous.spread(step, *due())
        slot += 1


def rms_parts(values):
    inverse = lax.rsqrt(jnp.mean(values * values, axis=-1, keepdims=True) + EPS)
    return values * inverse, inverse


def rms_backward(grad_normed, unit_rows, inverse, norm_gain):
    scaled = grad_normed * norm_gain
    grad_rows = inverse * (
        scaled - unit_rows * jnp.mean(scaled * unit_rows, axis=-1, keepdims=True)
    )
    return jnp.sum(grad_normed * unit_rows, axis=0), grad_rows


def rotate(values, cosine, sine):
    half = values.shape[1] // 2
    a, b = values[:, :half], values[:, half:]
    return jnp.concatenate([a * cosine - b * sine, b * cosine + a * sine], axis=1)


def rotate_back(grads, cosine, sine):
    half = grads.shape[1] // 2
    a, b = grads[:, :half], grads[:, half:]
    return jnp.concatenate([a * cosine + b * sine, b * cosine - a * sine], axis=1)


def per_device(
    tokens, doc_starts, gain_one, w_query, w_key, w_value, w_out, gain_two, w_gate, w_up, w_down,
    cotangent,
):
    n_z, n_c, n_f = lax.axis_size("z"), lax.axis_size("core"), lax.axis_size("f")
    z, c, f = lax.axis_index("z"), lax.axis_index("core"), lax.axis_index("f")
    n_t = n_f * n_c
    block_len, width = tokens.shape[3], tokens.shape[4]
    rows = 2 * block_len
    plane, span = n_t * rows, n_c * rows
    shard = width // n_f
    q_width = w_query.shape[1] // n_t
    kv_width = w_key.shape[1] // n_t
    hidden = w_gate.shape[1] // n_t
    qkv_width = q_width + 2 * kv_width
    heads = q_width // HEAD_SIZE
    in_plane = ("f", "core")

    own_x = tokens.reshape(rows, width)
    own_dy = cotangent.reshape(rows, width)

    z_order = [(z - s) % n_z for s in range(n_z)]

    order = Order()
    do = order.region

    first = do(
        payload,
        own_x, doc_starts.reshape(1, rows), gain_one.reshape(1, shard), gain_two.reshape(1, shard),
    )
    payloads = lax.all_gather(first, in_plane, axis=0, tiled=True)

    w_qkv = do(lambda *w: pack_qkv(*w, c, n_f, n_c), w_query, w_key, w_value)
    w_qkv = lax.all_to_all(with_layout_constraint(w_qkv, Layout((0, 1, 2))), "f", 0, 0)
    w_qkv = with_layout_constraint(w_qkv, Layout((0, 1, 2)))
    gate_parts, up_parts = do(
        lambda *w: [slice_columns(x, c, n_f, n_c) for x in w], w_gate, w_up
    )

    def project(payloads, w_qkv):
        gains = payloads.reshape(n_f, n_c, rows + EXTRA, width)[:, 0, rows + 2 : rows + 4, :shard]
        gains = jnp.transpose(gains, (1, 0, 2)).reshape(2, width).astype(F32)
        w_qkv = w_qkv.reshape(width, qkv_width)
        return (gains, w_qkv) + tuple(
            project_first(payloads, gains, w_qkv, z, n_z, n_c, block_len)
        )

    payloads, w_qkv = order.pin(payloads, w_qkv)
    gate_full = lax.all_to_all(
        lax.optimization_barrier((gate_parts, w_qkv))[0], "f", 0, 0
    )
    gains, w_qkv, h_one, query, key_value, cosine, sine, starts = do(project, payloads, w_qkv)
    gain_one_full, gain_two_full = gains[0], gains[1]
    starts = starts.reshape(n_f, 1, span)
    (early_dy,) = order.pin(own_dy)
    dy_all = lax.all_gather(early_dy, in_plane, axis=0, tiled=True)

    def positions(z_index):
        device = z_index * n_c + jnp.arange(n_c, dtype=jnp.int32)[:, None]
        within = jnp.arange(rows, dtype=jnp.int32)[None, :]
        return jnp.where(
            within < block_len,
            device * block_len + within,
            (2 * n_z * n_c - 1 - device) * block_len + within - block_len,
        ).reshape(span)

    q_pos = positions(z)[None, :]
    k_pos = jnp.concatenate([positions(zi) for zi in z_order])[:, None]

    key_values = turn_along_z(key_value)
    attn, attn_low, lse = do(
        lambda query, *kvs: attention(query, kvs, k_pos, q_pos, starts, n_f), query, *key_values
    )
    def reduce_plane(value):
        return lax.psum_scatter(value, in_plane, scatter_dimension=0, tiled=True)

    residual = own_x.astype(F32)
    def project_out(attn_low, w_out, gate_full):
        rows_of = lax.dynamic_slice_in_dim(w_out, c * q_width, q_width, 0)
        return rows_of, tn(attn_low, rows_of).astype(BF16), gate_full

    out_rows, projected, gate_full = do(project_out, attn_low, w_out, gate_full)
    (up_parts,) = order.pin(up_parts)
    up_full = lax.all_to_all(up_parts, "f", 0, 0).reshape(width, hidden)
    gate_full = gate_full.reshape(width, hidden)

    def after_attention(reduced, up_full):
        middle = residual + reduced.astype(F32)
        unit, inverse = rms_parts(middle)
        return middle, unit, inverse, (unit * gain_two_full).astype(BF16), up_full

    middle, unit_two, inv_two, h_two, up_full = do(
        after_attention, reduce_plane(projected), up_full
    )
    h_two = lax.all_gather(h_two, in_plane, axis=0, tiled=True)

    def forward(h_two, gate_full, up_full):
        gate, up = nn(h_two, gate_full), nn(h_two, up_full)
        return gate, up, (gate * jax.nn.sigmoid(gate) * up).astype(BF16)

    gate, up, mid = do(forward, h_two, gate_full, up_full)
    down_rows = do(lambda w: lax.dynamic_slice_in_dim(w, c * hidden, hidden, 0), w_down)

    def work(dy, down_rows, gate, up):
        sigmoid = jax.nn.sigmoid(gate)
        grad_mid = nt(dy, down_rows)
        grad_g = (grad_mid * up * sigmoid * (1.0 + gate * (1.0 - sigmoid))).astype(BF16)
        return grad_g, (grad_mid * (gate * sigmoid)).astype(BF16)

    grad_down = do(lambda mid, dy: tn(mid, dy).astype(BF16), mid, dy_all)
    sum_down = ZSum(grad_down.reshape(n_z, hidden // n_z, width), 0)
    sum_down.add(1)
    grad_g, grad_u = do(work, after(dy_all, *sum_down.sent), down_rows, gate, up)
    sum_down.add(2, grad_g, grad_u)
    h_two_parts = do(
        lambda g, u: (nt(g, gate_full) + nt(u, up_full)).astype(BF16),
        after(grad_g, *sum_down.sent), grad_u,
    )
    h_two_back = reduce_plane(h_two_parts)
    for step in range(3, n_z):
        sum_down.add(step, h_two_parts)
    sum_down.close()
    sum_down.spread(1)
    h_two_back = after(h_two_back, sum_down.own)

    grad_gate = tn(h_two, grad_g).astype(BF16)
    grad_up = tn(h_two, grad_u).astype(BF16)
    grad_gain_two, grad_norm = rms_backward(
        h_two_back.astype(F32), unit_two, inv_two, gain_two_full
    )
    grad_middle = own_dy.astype(F32) + grad_norm

    branch_low = grad_middle.astype(BF16)
    grad_branch = lax.all_gather(branch_low, in_plane, axis=0, tiled=True)
    grad_attn = nt(out_rows, grad_branch).astype(BF16)
    grad_out = nn(attn_low, grad_branch).astype(BF16)
    grad_query, grad_kv = attention_back(
        query, key_values, grad_attn, attn, lse, k_pos, q_pos, starts, n_f, z_order
    )
    kv_total = jnp.sum(lax.all_to_all(grad_kv, "z", 0, 0).astype(F32), axis=0)
    grad_query = grad_query.reshape(heads, HEAD_SIZE, plane) * HEAD_SIZE ** (-0.5)
    grad_qkv = jnp.concatenate(
        [
            rotate_back(grad_query, cosine, sine).reshape(q_width, plane),
            rotate_back(kv_total[None, :HEAD_SIZE], cosine, sine)[0],
            kv_total[HEAD_SIZE:],
        ],
        axis=0,
    ).astype(BF16)
    grad_w_qkv = lax.dot_general(
        h_one, grad_qkv, (((0,), (1,)), ((), ())), preferred_element_type=F32
    ).astype(BF16)
    h_one_parts = lax.dot_general(
        grad_qkv, w_qkv, (((0,), (1,)), ((), ())), preferred_element_type=F32
    ).astype(BF16)
    mixed_parts = nn(mid, down_rows).astype(BF16)
    mixed = middle + reduce_plane(after(mixed_parts, grad_branch)).astype(F32)
    grad_h_one = reduce_plane(h_one_parts).astype(F32)
    unit_one, inv_one = rms_parts(residual)
    grad_gain_one, grad_norm = rms_backward(grad_h_one, unit_one, inv_one, gain_one_full)
    grad_tokens = grad_middle + grad_norm
    gains = jnp.stack([grad_gain_one, grad_gain_two])
    for axis, size in (("z", n_z), ("f", n_f), ("core", n_c)):
        for bit in range(size.bit_length() - 1):
            gains = gains + swap(gains, axis, 1 << bit)
    gain_grads = lax.dynamic_slice_in_dim(gains, f * shard, shard, 1)

    def to_shards(grad):
        return lax.all_to_all(grad, "f", 0, 0)

    def by_z(grad, axis):
        shape = grad.shape
        return grad.reshape(shape[:axis] + (n_z, shape[axis] // n_z) + shape[axis + 1 :])

    gate_shards = to_shards(grad_gate.reshape(n_f, shard, hidden))
    up_shards = to_shards(after(grad_up.reshape(n_f, shard, hidden), gate_shards))
    sum_gate = ZSum(by_z(gate_shards, 1), 1)
    sum_up = ZSum(by_z(up_shards, 1), 1)
    sum_out = ZSum(by_z(grad_out, 0), 0)
    sum_qkv = ZSum(by_z(to_shards(grad_w_qkv.reshape(n_f, shard, qkv_width)), 1), 1)
    def finish_rows(one):
        cores = one.result()
        piece_rows, columns = cores[0].shape[1:]
        if piece_rows % 8 == 0:
            return assemble_rows(cores, c)
        result = blank((n_c, n_z, piece_rows, columns), F32)
        for e, piece in enumerate(cores):
            result = lax.dynamic_update_index_in_dim(result, piece.astype(F32), c ^ e, 0)
        return result.reshape(-1, columns)

    def finish_columns(one, splits):
        cores = one.result()
        piece_rows = cores[0].shape[2]
        if piece_rows % 8 == 0:
            return assemble(cores, c, splits)
        results = []
        for low, high in splits:
            out = blank((n_z, piece_rows, n_f, n_c, high - low), F32)
            for e, piece in enumerate(cores):
                update = jnp.transpose(piece[..., low:high].astype(F32), (0, 2, 1, 3))
                out = lax.dynamic_update_index_in_dim(out, update, c ^ e, 3)
            results.append(out.reshape(shard, n_t * (high - low)))
        return results

    totals = {}

    def finish(name, function, *args):
        def get():
            if name not in totals:
                made = function(*args)
                totals[name] = made if isinstance(made, (list, tuple)) else [made]
            return totals[name]

        return get

    down_done = finish("down", finish_rows, sum_down)
    gate_done = finish("gate", finish_columns, sum_gate, [(0, hidden)])
    up_done = finish("up", finish_columns, sum_up, [(0, hidden)])
    out_done = finish("out", finish_rows, sum_out)
    splits = [(0, q_width), (q_width, q_width + kv_width), (q_width + kv_width, qkv_width)]
    qkv_done = finish("qkv", finish_columns, sum_qkv, splits)

    def slot(which, step):
        return which * n_z + min(step, n_z - 1)

    run_sums(
        sum_down,
        [sum_gate, sum_up, sum_out, sum_qkv],
        {
            slot(2, 0): lambda: [grad_kv],
            slot(2, 2): lambda: [grad_qkv],
            slot(2, 3): lambda: [grad_w_qkv, h_one_parts],
            slot(3, 0): down_done,
            slot(3, 2): gate_done,
            slot(4, 2): lambda: [*up_done(), gain_grads],
            slot(4, 3): out_done,
        },
    )
    total_down, total_gate, total_up, total_out = (
        done()[0] for done in (down_done, gate_done, up_done, out_done)
    )
    total_query, total_key, total_value = qkv_done()
    return (
        mixed.reshape(tokens.shape),
        grad_tokens.reshape(tokens.shape),
        gain_grads[0],
        total_query,
        total_key,
        total_value,
        total_out,
        gain_grads[1],
        total_gate,
        total_up,
        total_down,
    )


def solution(mesh):
    n_ctx, n_fsdp = mesh.shape["ctx"], mesh.shape["fsdp"]
    n_core = KEY_VALUE_HEADS // n_fsdp
    inner = Mesh(
        np.asarray(mesh.devices).reshape(n_ctx // n_core, n_core, n_fsdp), ("z", "core", "f")
    )
    ctx = ("z", "core")
    return jax.shard_map(
        per_device,
        mesh=inner,
        in_specs=(
            P("f", ctx, None, None, None),
            P("f", ctx, None, None),
            P("f"),
            P("f", None),
            P("f", None),
            P("f", None),
            P("f", None),
            P("f"),
            P("f", None),
            P("f", None),
            P("f", None),
            P("f", ctx, None, None, None),
        ),
        out_specs=(
            P("f", ctx, None, None, None),
            P("f", ctx, None, None, None),
            P("f"),
            P("f", None),
            P("f", None),
            P("f", None),
            P("f", None),
            P("f"),
            P("f", None),
            P("f", None),
            P("f", None),
        ),
        check_vma=False,
    )
```

```python
import jax
import jax.numpy as jnp
import numpy as np
from jax import lax
from jax.experimental import pallas as pl
from jax.experimental.layout import Layout, with_layout_constraint
from jax.experimental.pallas import tpu as pltpu
from jax.sharding import Mesh
from jax.sharding import PartitionSpec as P

QUERY_HEADS = 32
KEY_VALUE_HEADS = 8
HEAD_SIZE = 80

EPS = 1e-05
THETA = 1000000.0
NEGATIVE_LARGE = -1e30

F32 = jnp.float32
BF16 = jnp.bfloat16

ANY = pl.BlockSpec(memory_space=pl.ANY)
PARAMS = pltpu.CompilerParams(vmem_limit_bytes=56 * 1024 * 1024)


class Order:
    def __init__(self):
        self.last = ()

    def pin(self, *arrays):
        return lax.optimization_barrier(arrays + self.last)[: len(arrays)]

    def region(self, function, *arrays):
        results = function(*self.pin(*arrays))
        single = not isinstance(results, (tuple, list))
        self.last = (results,) if single else tuple(results)
        return results


def scalars(*values):
    return jnp.stack([jnp.asarray(v, jnp.int32) for v in values])


def moved(*arrays):
    return pl.CostEstimate(
        flops=0, transcendentals=0, bytes_accessed=2 * sum(a.size * a.dtype.itemsize for a in arrays)
    )


def whole(shape):
    return pl.BlockSpec(shape, lambda *_: (0,) * len(shape))


def blank(shape, dtype):
    return pl.pallas_call(
        lambda out: None, out_shape=jax.ShapeDtypeStruct(shape, dtype), out_specs=ANY
    )()


def swap(value, axis, offset):
    size = lax.axis_size(axis)
    return lax.ppermute(value, axis, [(i, i ^ offset) for i in range(size)])


def pack_qkv(w_query, w_key, w_value, core, n_f, n_c):
    rows = w_query.shape[0]
    n_t = n_f * n_c
    q, kv = w_query.shape[1] // n_t, w_key.shape[1] // n_t

    def body(where, wq, wk, wv, out):
        for c in range(n_c):

            @pl.when(where[0] == c)
            def _(c=c):
                for f in range(n_f):
                    t = f * n_c + c
                    out[f, :, :q] = wq[:, t * q : (t + 1) * q]
                    out[f, :, q : q + kv] = wk[:, t * kv : (t + 1) * kv]
                    out[f, :, q + kv :] = wv[:, t * kv : (t + 1) * kv]

    block = rows // 4
    return pl.pallas_call(
        body,
        out_shape=jax.ShapeDtypeStruct((n_f, rows, q + 2 * kv), BF16),
        grid_spec=pltpu.PrefetchScalarGridSpec(
            num_scalar_prefetch=1,
            grid=(4,),
            in_specs=[
                pl.BlockSpec((block, w.shape[1]), lambda i, where: (i, 0))
                for w in (w_query, w_key, w_value)
            ],
            out_specs=pl.BlockSpec((n_f, block, q + 2 * kv), lambda i, where: (0, i, 0)),
        ),
        compiler_params=PARAMS,
        cost_estimate=moved(w_query),
    )(scalars(core), w_query, w_key, w_value)


def slice_columns(weight, core, n_f, n_c):
    rows, size = weight.shape[0], weight.shape[1] // (n_f * n_c)

    def body(where, source, out):
        out[0] = source[...]

    return pl.pallas_call(
        body,
        out_shape=jax.ShapeDtypeStruct((n_f, rows, size), weight.dtype),
        grid_spec=pltpu.PrefetchScalarGridSpec(
            num_scalar_prefetch=1,
            grid=(n_f,),
            in_specs=[pl.BlockSpec((rows, size), lambda i, where: (0, i * n_c + where[0]))],
            out_specs=pl.BlockSpec((1, rows, size), lambda i, where: (i, 0, 0)),
        ),
        compiler_params=PARAMS,
        cost_estimate=moved(weight),
    )(scalars(core), weight)


EXTRA = 32
DIGIT = 64


def payload(x, starts, gain_one, gain_two):
    rows, width = x.shape

    def body(x, starts, one, two, out):
        out[:rows] = x[...]
        out[rows : rows + EXTRA] = jnp.zeros((EXTRA, width), BF16)
        low = (starts[...] & (DIGIT - 1)).astype(F32)
        high = (starts[...] // DIGIT).astype(F32)
        for row, value in enumerate((low, high, one[...].astype(F32), two[...].astype(F32))):
            out[rows + row : rows + row + 1, : value.shape[1]] = value.astype(BF16)

    return pl.pallas_call(
        body,
        out_shape=jax.ShapeDtypeStruct((rows + EXTRA, width), BF16),
        compiler_params=PARAMS,
        cost_estimate=moved(x),
    )(x, starts, gain_one, gain_two)


def project_first(payloads, gains, w_qkv, z, n_z, n_c, block_len):
    width, columns = w_qkv.shape
    rows = 2 * block_len
    count = payloads.shape[0] // (rows + EXTRA)
    half = HEAD_SIZE // 2
    q_width = columns - 2 * HEAD_SIZE
    inv_freq = THETA ** (-(jnp.arange(half, dtype=F32) * 2.0) / HEAD_SIZE)

    def body(where, block, gain, w, freq, h_out, q_out, kv_out, cos_out, sin_out, st_out):
        x = block[:rows].astype(F32)
        inverse = lax.rsqrt(jnp.mean(x * x, axis=-1, keepdims=True) + EPS)
        h_out[...] = (x * inverse * gain[0:1]).astype(BF16)
        low, high = block[rows : rows + 1, :rows], block[rows + 1 : rows + 2, :rows]
        start = (low.astype(F32) + high.astype(F32) * DIGIT).astype(jnp.int32)
        st_out[0] = start
        device = where[0] * n_c + lax.rem(pl.program_id(0), n_c)
        within = lax.broadcasted_iota(jnp.int32, (1, rows), 1)
        position = jnp.where(
            within < block_len,
            device * block_len + within,
            (2 * n_z * n_c - 1 - device) * block_len + within - block_len,
        )
        angles = freq[...] * (position - start).astype(F32)
        cosine, sine = jnp.cos(angles), jnp.sin(angles)
        cos_out[...] = cosine
        sin_out[...] = sine
        projected = nn(h_out[...], w[...]).T

        def turned(row):
            a, b = projected[row : row + half], projected[row + half : row + HEAD_SIZE]
            return jnp.concatenate([a * cosine - b * sine, b * cosine + a * sine], axis=0)

        for row in range(0, q_width, HEAD_SIZE):
            q_out[row : row + HEAD_SIZE] = (turned(row) * HEAD_SIZE ** (-0.5)).astype(BF16)
        kv_out[:HEAD_SIZE] = turned(q_width).astype(BF16)
        kv_out[HEAD_SIZE:] = projected[q_width + HEAD_SIZE :].astype(BF16)

    tokens = count * rows

    def lanes(size):
        return pl.BlockSpec((size, rows), lambda g, where: (0, g))

    return pl.pallas_call(
        body,
        out_shape=[
            jax.ShapeDtypeStruct((tokens, width), BF16),
            jax.ShapeDtypeStruct((q_width, tokens), BF16),
            jax.ShapeDtypeStruct((2 * HEAD_SIZE, tokens), BF16),
            jax.ShapeDtypeStruct((half, tokens), F32),
            jax.ShapeDtypeStruct((half, tokens), F32),
            jax.ShapeDtypeStruct((count, 1, rows), jnp.int32),
        ],
        grid_spec=pltpu.PrefetchScalarGridSpec(
            num_scalar_prefetch=1,
            grid=(count,),
            in_specs=[
                pl.BlockSpec((rows + EXTRA, width), lambda g, where: (g, 0)),
                whole(gains.shape),
                whole(w_qkv.shape),
                whole((half, 1)),
            ],
            out_specs=[
                pl.BlockSpec((rows, width), lambda g, where: (g, 0)),
                lanes(q_width),
                lanes(2 * HEAD_SIZE),
                lanes(half),
                lanes(half),
                pl.BlockSpec((1, 1, rows), lambda g, where: (g, 0, 0)),
            ],
        ),
        compiler_params=PARAMS,
        cost_estimate=pl.CostEstimate(
            flops=2 * tokens * width * columns,
            transcendentals=tokens * HEAD_SIZE,
            bytes_accessed=4 * tokens * width,
        ),
    )(scalars(z), payloads, gains, w_qkv, inv_freq[:, None])


def tn(a, b):
    return lax.dot_general(a, b, (((0,), (0,)), ((), ())), preferred_element_type=F32)


def nt(a, b):
    return lax.dot_general(a, b, (((1,), (1,)), ((), ())), preferred_element_type=F32)


def nn(a, b):
    return lax.dot_general(a, b, (((1,), (0,)), ((), ())), preferred_element_type=F32)


def visible_rows(k_pos, q_pos, starts):
    return (k_pos >= starts) & (k_pos <= q_pos)


def attention(query, key_values, k_pos, q_pos, starts, n_f):
    width, tokens = query.shape
    heads, span, n_z = width // HEAD_SIZE, tokens // n_f, len(key_values)

    def body(*refs):
        q, kvs = refs[0], refs[1 : 1 + n_z]
        kp, qp, st, out, low, lse = refs[1 + n_z :]
        keys = jnp.concatenate([kv[:HEAD_SIZE] for kv in kvs], axis=1)
        values = jnp.concatenate([kv[HEAD_SIZE:] for kv in kvs], axis=1)
        seen = visible_rows(kp[...], qp[...], st[0])
        for h in range(heads):
            part = slice(h * HEAD_SIZE, (h + 1) * HEAD_SIZE)
            scores = jnp.where(seen, tn(keys, q[part]), NEGATIVE_LARGE)
            top = jnp.max(scores, axis=0, keepdims=True)
            terms = jnp.exp(scores - top)
            total = jnp.sum(terms, axis=0, keepdims=True)
            result = nn(values, terms.astype(BF16)) / total
            out[part] = result
            low[part] = result.astype(BF16)
            lse[0, h : h + 1] = top + jnp.log(total)

    return pl.pallas_call(
        body,
        out_shape=[
            jax.ShapeDtypeStruct((width, tokens), F32),
            jax.ShapeDtypeStruct((width, tokens), BF16),
            jax.ShapeDtypeStruct((n_f, heads, span), F32),
        ],
        grid=(n_f,),
        in_specs=[pl.BlockSpec((width, span), lambda i: (0, i))]
        + [pl.BlockSpec((2 * HEAD_SIZE, span), lambda i: (0, i))] * n_z
        + [
            whole(k_pos.shape),
            whole(q_pos.shape),
            pl.BlockSpec((1, 1, span), lambda i: (i, 0, 0)),
        ],
        out_specs=[
            pl.BlockSpec((width, span), lambda i: (0, i)),
            pl.BlockSpec((width, span), lambda i: (0, i)),
            pl.BlockSpec((1, heads, span), lambda i: (i, 0, 0)),
        ],
        compiler_params=PARAMS,
        cost_estimate=pl.CostEstimate(
            flops=4 * width * tokens * span * n_z,
            transcendentals=heads * tokens * span * n_z,
            bytes_accessed=8 * width * tokens,
        ),
    )(query, *key_values, k_pos, q_pos, starts)


def attention_back(query, key_values, grad, out, lse, k_pos, q_pos, starts, n_f, z_order):
    width, tokens = query.shape
    heads, span, n_z = width // HEAD_SIZE, tokens // n_f, len(key_values)

    def body(where, *refs):
        q, kvs = refs[0], refs[1 : 1 + n_z]
        do, o, l, kp, qp, st, dq = refs[1 + n_z : 8 + n_z]
        dkv = refs[8 + n_z]
        keys = jnp.concatenate([kv[:HEAD_SIZE] for kv in kvs], axis=1)
        values = jnp.concatenate([kv[HEAD_SIZE:] for kv in kvs], axis=1)
        seen = visible_rows(kp[...], qp[...], st[0])
        grad_keys = jnp.zeros((HEAD_SIZE, n_z * span), F32)
        grad_values = jnp.zeros((HEAD_SIZE, n_z * span), F32)
        for h in range(heads):
            part = slice(h * HEAD_SIZE, (h + 1) * HEAD_SIZE)
            scores = jnp.where(seen, tn(keys, q[part]), NEGATIVE_LARGE)
            probs = jnp.exp(scores - l[0, h : h + 1])
            delta = jnp.sum(do[part].astype(F32) * o[part], axis=0, keepdims=True)
            grad_values += nt(do[part], probs.astype(BF16))
            grad_scores = (probs * (tn(values, do[part]) - delta)).astype(BF16)
            dq[part] = nn(keys, grad_scores)
            grad_keys += nt(q[part], grad_scores)
        for s in range(n_z):
            here = slice(s * span, (s + 1) * span)
            dkv[where[s], :HEAD_SIZE] = grad_keys[:, here].astype(BF16)
            dkv[where[s], HEAD_SIZE:] = grad_values[:, here].astype(BF16)

    wide = pl.BlockSpec((width, span), lambda i, where: (0, i))
    narrow = pl.BlockSpec((2 * HEAD_SIZE, span), lambda i, where: (0, i))
    return pl.pallas_call(
        body,
        out_shape=[
            jax.ShapeDtypeStruct((width, tokens), F32),
            jax.ShapeDtypeStruct((n_z, 2 * HEAD_SIZE, tokens), BF16),
        ],
        grid_spec=pltpu.PrefetchScalarGridSpec(
            num_scalar_prefetch=1,
            grid=(n_f,),
            in_specs=[wide]
            + [narrow] * n_z
            + [
                wide,
                wide,
                pl.BlockSpec((1, heads, span), lambda i, where: (i, 0, 0)),
                whole(k_pos.shape),
                whole(q_pos.shape),
                pl.BlockSpec((1, 1, span), lambda i, where: (i, 0, 0)),
            ],
            out_specs=[
                wide,
                pl.BlockSpec((n_z, 2 * HEAD_SIZE, span), lambda i, where: (0, 0, i)),
            ],
        ),
        compiler_params=PARAMS,
        cost_estimate=pl.CostEstimate(
            flops=10 * width * tokens * span * n_z,
            transcendentals=heads * tokens * span * n_z,
            bytes_accessed=12 * width * tokens,
        ),
    )(scalars(*z_order), query, *key_values, grad, out, lse, k_pos, q_pos, starts)


def collect(own, ups, downs, z):
    shape = own.shape
    n_z = len(ups) + 1
    zeros = (0,) * len(shape)

    def body(where, *refs):
        out = refs[2 * n_z - 1]
        k = pl.program_id(0)

        @pl.when(k == where[0])
        def _():
            out[0] = refs[0][...]

        for s in range(1, n_z):

            @pl.when(where[0] - k == s)
            def _(s=s):
                out[0] = refs[s][...]

            @pl.when(k - where[0] == s)
            def _(s=s):
                out[0] = refs[n_z - 1 + s][...]

    return pl.pallas_call(
        body,
        out_shape=jax.ShapeDtypeStruct((n_z,) + shape, own.dtype),
        grid_spec=pltpu.PrefetchScalarGridSpec(
            num_scalar_prefetch=1,
            grid=(n_z,),
            in_specs=[whole(shape)] * (2 * n_z - 1),
            out_specs=pl.BlockSpec((1,) + shape, lambda g, where: (g,) + zeros),
        ),
        compiler_params=PARAMS,
        cost_estimate=moved(*[own] * n_z),
    )(scalars(z), own, *ups, *downs)


def assemble(cores, core, splits):
    n_c = len(cores)
    n_z, n_f, rows, columns = cores[0].shape
    n_t = n_f * n_c

    def body(where, *refs):
        outs = refs[n_c:]
        for own in range(n_c):

            @pl.when(where[0] == own)
            def _(own=own):
                for e in range(n_c):
                    for i in range(n_f):
                        t = i * n_c + (own ^ e)
                        part = refs[e][0, i].astype(F32)
                        for out, (low, high) in zip(outs, splits, strict=True):
                            size = high - low
                            out[:, t * size : (t + 1) * size] = part[:, low:high]

    return pl.pallas_call(
        body,
        out_shape=[
            jax.ShapeDtypeStruct((n_z * rows, n_t * (high - low)), F32) for low, high in splits
        ],
        grid_spec=pltpu.PrefetchScalarGridSpec(
            num_scalar_prefetch=1,
            grid=(n_z,),
            in_specs=[
                pl.BlockSpec((1, n_f, rows, columns), lambda g, where: (g, 0, 0, 0))
                for _ in cores
            ],
            out_specs=[
                pl.BlockSpec((rows, n_t * (high - low)), lambda g, where: (g, 0))
                for low, high in splits
            ],
        ),
        compiler_params=PARAMS,
        cost_estimate=moved(*cores),
    )(scalars(core), *cores)


def assemble_rows(cores, core):
    n_c = len(cores)
    n_z, rows, columns = cores[0].shape

    def body(where, *refs):
        for e in range(n_c):

            @pl.when(pl.program_id(0) == e)
            def _(e=e):
                refs[n_c][...] = refs[e][0].astype(F32)

    def in_map(e):
        return lambda g, k, where: (jnp.clip(k + (g - e) * n_z, 0, n_z - 1), 0, 0)

    return pl.pallas_call(
        body,
        out_shape=jax.ShapeDtypeStruct((n_c * n_z * rows, columns), F32),
        grid_spec=pltpu.PrefetchScalarGridSpec(
            num_scalar_prefetch=1,
            grid=(n_c, n_z),
            in_specs=[pl.BlockSpec((1, rows, columns), in_map(e)) for e in range(n_c)],
            out_specs=pl.BlockSpec(
                (rows, columns), lambda g, k, where: ((where[0] ^ g) * n_z + k, 0)
            ),
        ),
        compiler_params=PARAMS,
        cost_estimate=moved(*cores),
    )(scalars(core), *cores)


def turn_along_z(own):
    n_z = lax.axis_size("z")
    return [own] + [
        lax.ppermute(own, "z", [(i, (i + s) % n_z) for i in range(n_z)]) for s in range(1, n_z)
    ]


def after(value, *earlier):
    return lax.optimization_barrier((value,) + earlier)[0]


class ZSum:
    def __init__(self, parts, z_axis, between=None):
        self.parts, self.z_axis, self.between = parts, z_axis, between
        self.n_z, self.z = lax.axis_size("z"), lax.axis_index("z")
        self.up = self.down = None

    def chunk(self, k):
        k = jnp.clip(k, 0, self.n_z - 1)
        return lax.dynamic_index_in_dim(self.parts, k, self.z_axis, keepdims=False)

    def add(self, step, *earlier):
        n_z = self.n_z
        up, down = self.chunk(self.z + n_z - step), self.chunk(self.z - n_z + step)
        if self.up is not None:
            up = (up.astype(F32) + self.up.astype(F32)).astype(BF16)
            down = (down.astype(F32) + self.down.astype(F32)).astype(BF16)
        if earlier:
            up, down = after(up, *earlier), after(down, *earlier)
        self.sent = (up, down)
        self.up = lax.ppermute(up, "z", [(i, i + 1) for i in range(step)])
        self.down = lax.ppermute(down, "z", [(i, i - 1) for i in range(n_z - step, n_z)])

    def close(self):
        total = self.chunk(self.z).astype(F32)
        total = (total + self.up.astype(F32) + self.down.astype(F32)).astype(BF16)
        self.own = total if self.between is None else self.between(total)
        self.ups, self.downs = [self.own], [self.own]

    def spread(self, step, *earlier):
        n_z = self.n_z
        up, down = self.ups[-1], self.downs[-1]
        if earlier:
            up, down = after(up, *earlier), after(down, *earlier)
        self.ups.append(lax.ppermute(up, "z", [(i, i + 1) for i in range(step - 1, n_z - 1)]))
        self.downs.append(lax.ppermute(down, "z", [(i, i - 1) for i in range(1, n_z - step + 1)]))

    def result(self):
        mine = collect(self.own, self.ups[1:], self.downs[1:], self.z)
        return [mine] + [swap(mine, "core", e) for e in range(1, lax.axis_size("core"))]


def run_sums(previous, sums, waits):
    slot = previous.n_z

    def due():
        return tuple(waits[slot]()) if slot in waits else ()

    for one in sums:
        n_z = one.n_z
        for step in range(1, n_z):
            one.add(step, *due(), previous.ups[step], previous.downs[step])
            if step + 1 < n_z:
                previous.spread(step + 1)
            slot += 1
        one.close()
        one.spread(1, *due())
        slot += 1
        previous = one
    for step in range(2, previous.n_z):
        previous.spread(step, *due())
        slot += 1


def rms_parts(values):
    inverse = lax.rsqrt(jnp.mean(values * values, axis=-1, keepdims=True) + EPS)
    return values * inverse, inverse


def rms_backward(grad_normed, unit_rows, inverse, norm_gain):
    scaled = grad_normed * norm_gain
    grad_rows = inverse * (
        scaled - unit_rows * jnp.mean(scaled * unit_rows, axis=-1, keepdims=True)
    )
    return jnp.sum(grad_normed * unit_rows, axis=0), grad_rows


def rotate(values, cosine, sine):
    half = values.shape[1] // 2
    a, b = values[:, :half], values[:, half:]
    return jnp.concatenate([a * cosine - b * sine, b * cosine + a * sine], axis=1)


def rotate_back(grads, cosine, sine):
    half = grads.shape[1] // 2
    a, b = grads[:, :half], grads[:, half:]
    return jnp.concatenate([a * cosine + b * sine, b * cosine - a * sine], axis=1)


def per_device(
    tokens, doc_starts, gain_one, w_query, w_key, w_value, w_out, gain_two, w_gate, w_up, w_down,
    cotangent,
):
    n_z, n_c, n_f = lax.axis_size("z"), lax.axis_size("core"), lax.axis_size("f")
    z, c, f = lax.axis_index("z"), lax.axis_index("core"), lax.axis_index("f")
    n_t = n_f * n_c
    block_len, width = tokens.shape[3], tokens.shape[4]
    rows = 2 * block_len
    plane, span = n_t * rows, n_c * rows
    shard = width // n_f
    q_width = w_query.shape[1] // n_t
    kv_width = w_key.shape[1] // n_t
    hidden = w_gate.shape[1] // n_t
    qkv_width = q_width + 2 * kv_width
    heads = q_width // HEAD_SIZE
    in_plane = ("f", "core")

    own_x = tokens.reshape(rows, width)
    own_dy = cotangent.reshape(rows, width)

    z_order = [(z - s) % n_z for s in range(n_z)]

    order = Order()
    do = order.region

    first = do(
        payload,
        own_x, doc_starts.reshape(1, rows), gain_one.reshape(1, shard), gain_two.reshape(1, shard),
    )
    payloads = lax.all_gather(first, in_plane, axis=0, tiled=True)

    w_qkv = do(lambda *w: pack_qkv(*w, c, n_f, n_c), w_query, w_key, w_value)
    w_qkv = lax.all_to_all(with_layout_constraint(w_qkv, Layout((0, 1, 2))), "f", 0, 0)
    w_qkv = with_layout_constraint(w_qkv, Layout((0, 1, 2)))
    gate_parts, up_parts = do(
        lambda *w: [slice_columns(x, c, n_f, n_c) for x in w], w_gate, w_up
    )

    def project(payloads, w_qkv):
        gains = payloads.reshape(n_f, n_c, rows + EXTRA, width)[:, 0, rows + 2 : rows + 4, :shard]
        gains = jnp.transpose(gains, (1, 0, 2)).reshape(2, width).astype(F32)
        w_qkv = w_qkv.reshape(width, qkv_width)
        return (gains, w_qkv) + tuple(
            project_first(payloads, gains, w_qkv, z, n_z, n_c, block_len)
        )

    payloads, w_qkv = order.pin(payloads, w_qkv)
    gate_full = lax.all_to_all(
        lax.optimization_barrier((gate_parts, w_qkv))[0], "f", 0, 0
    )
    gains, w_qkv, h_one, query, key_value, cosine, sine, starts = do(project, payloads, w_qkv)
    gain_one_full, gain_two_full = gains[0], gains[1]
    starts = starts.reshape(n_f, 1, span)
    (early_dy,) = order.pin(own_dy)
    dy_all = lax.all_gather(early_dy, in_plane, axis=0, tiled=True)

    def positions(z_index):
        device = z_index * n_c + jnp.arange(n_c, dtype=jnp.int32)[:, None]
        within = jnp.arange(rows, dtype=jnp.int32)[None, :]
        return jnp.where(
            within < block_len,
            device * block_len + within,
            (2 * n_z * n_c - 1 - device) * block_len + within - block_len,
        ).reshape(span)

    q_pos = positions(z)[None, :]
    k_pos = jnp.concatenate([positions(zi) for zi in z_order])[:, None]

    key_values = turn_along_z(key_value)
    attn, attn_low, lse = do(
        lambda query, *kvs: attention(query, kvs, k_pos, q_pos, starts, n_f), query, *key_values
    )
    def reduce_plane(value):
        return lax.psum_scatter(value, in_plane, scatter_dimension=0, tiled=True)

    residual = own_x.astype(F32)
    def project_out(attn_low, w_out, gate_full):
        rows_of = lax.dynamic_slice_in_dim(w_out, c * q_width, q_width, 0)
        return rows_of, tn(attn_low, rows_of).astype(BF16), gate_full

    out_rows, projected, gate_full = do(project_out, attn_low, w_out, gate_full)
    (up_parts,) = order.pin(up_parts)
    up_full = lax.all_to_all(up_parts, "f", 0, 0).reshape(width, hidden)
    gate_full = gate_full.reshape(width, hidden)

    def after_attention(reduced, up_full):
        middle = residual + reduced.astype(F32)
        unit, inverse = rms_parts(middle)
        return middle, unit, inverse, (unit * gain_two_full).astype(BF16), up_full

    middle, unit_two, inv_two, h_two, up_full = do(
        after_attention, reduce_plane(projected), up_full
    )
    h_two = lax.all_gather(h_two, in_plane, axis=0, tiled=True)

    def forward(h_two, gate_full, up_full):
        gate, up = nn(h_two, gate_full), nn(h_two, up_full)
        return gate, up, (gate * jax.nn.sigmoid(gate) * up).astype(BF16)

    gate, up, mid = do(forward, h_two, gate_full, up_full)
    down_rows = do(lambda w: lax.dynamic_slice_in_dim(w, c * hidden, hidden, 0), w_down)

    def work(dy, down_rows, gate, up):
        sigmoid = jax.nn.sigmoid(gate)
        grad_mid = nt(dy, down_rows)
        grad_g = (grad_mid * up * sigmoid * (1.0 + gate * (1.0 - sigmoid))).astype(BF16)
        return grad_g, (grad_mid * (gate * sigmoid)).astype(BF16)

    grad_down = do(lambda mid, dy: tn(mid, dy).astype(BF16), mid, dy_all)
    sum_down = ZSum(grad_down.reshape(n_z, hidden // n_z, width), 0)
    sum_down.add(1)
    grad_g, grad_u = do(work, after(dy_all, *sum_down.sent), down_rows, gate, up)
    sum_down.add(2, grad_g, grad_u)
    h_two_parts = do(
        lambda g, u: (nt(g, gate_full) + nt(u, up_full)).astype(BF16),
        after(grad_g, *sum_down.sent), grad_u,
    )
    h_two_back = reduce_plane(h_two_parts)
    for step in range(3, n_z):
        sum_down.add(step, h_two_parts)
    sum_down.close()
    sum_down.spread(1)
    h_two_back = after(h_two_back, sum_down.own)

    grad_gate = tn(h_two, grad_g).astype(BF16)
    grad_up = tn(h_two, grad_u).astype(BF16)
    grad_gain_two, grad_norm = rms_backward(
        h_two_back.astype(F32), unit_two, inv_two, gain_two_full
    )
    grad_middle = own_dy.astype(F32) + grad_norm

    branch_low = grad_middle.astype(BF16)
    grad_branch = lax.all_gather(branch_low, in_plane, axis=0, tiled=True)
    grad_attn = nt(out_rows, grad_branch).astype(BF16)
    grad_out = nn(attn_low, grad_branch).astype(BF16)
    grad_query, grad_kv = attention_back(
        query, key_values, grad_attn, attn, lse, k_pos, q_pos, starts, n_f, z_order
    )
    kv_total = jnp.sum(lax.all_to_all(grad_kv, "z", 0, 0).astype(F32), axis=0)
    grad_query = grad_query.reshape(heads, HEAD_SIZE, plane) * HEAD_SIZE ** (-0.5)
    grad_qkv = jnp.concatenate(
        [
            rotate_back(grad_query, cosine, sine).reshape(q_width, plane),
            rotate_back(kv_total[None, :HEAD_SIZE], cosine, sine)[0],
            kv_total[HEAD_SIZE:],
        ],
        axis=0,
    ).astype(BF16)
    grad_w_qkv = lax.dot_general(
        h_one, grad_qkv, (((0,), (1,)), ((), ())), preferred_element_type=F32
    ).astype(BF16)
    h_one_parts = lax.dot_general(
        grad_qkv, w_qkv, (((0,), (1,)), ((), ())), preferred_element_type=F32
    ).astype(BF16)
    mixed_parts = nn(mid, down_rows).astype(BF16)
    mixed = middle + reduce_plane(after(mixed_parts, grad_branch)).astype(F32)
    grad_h_one = reduce_plane(h_one_parts).astype(F32)
    unit_one, inv_one = rms_parts(residual)
    grad_gain_one, grad_norm = rms_backward(grad_h_one, unit_one, inv_one, gain_one_full)
    grad_tokens = grad_middle + grad_norm
    gains = jnp.stack([grad_gain_one, grad_gain_two])
    for axis, size in (("z", n_z), ("f", n_f), ("core", n_c)):
        for bit in range(size.bit_length() - 1):
            gains = gains + swap(gains, axis, 1 << bit)
    gain_grads = lax.dynamic_slice_in_dim(gains, f * shard, shard, 1)

    def to_shards(grad):
        return lax.all_to_all(grad, "f", 0, 0)

    def by_z(grad, axis):
        shape = grad.shape
        return grad.reshape(shape[:axis] + (n_z, shape[axis] // n_z) + shape[axis + 1 :])

    gate_shards = to_shards(grad_gate.reshape(n_f, shard, hidden))
    up_shards = to_shards(after(grad_up.reshape(n_f, shard, hidden), gate_shards))
    sum_gate = ZSum(by_z(gate_shards, 1), 1)
    sum_up = ZSum(by_z(up_shards, 1), 1)
    sum_out = ZSum(by_z(grad_out, 0), 0)
    sum_qkv = ZSum(by_z(to_shards(grad_w_qkv.reshape(n_f, shard, qkv_width)), 1), 1)
    def finish_rows(one):
        cores = one.result()
        piece_rows, columns = cores[0].shape[1:]
        if piece_rows % 8 == 0:
            return assemble_rows(cores, c)
        result = blank((n_c, n_z, piece_rows, columns), F32)
        for e, piece in enumerate(cores):
            result = lax.dynamic_update_index_in_dim(result, piece.astype(F32), c ^ e, 0)
        return result.reshape(-1, columns)

    def finish_columns(one, splits):
        cores = one.result()
        piece_rows = cores[0].shape[2]
        if piece_rows % 8 == 0:
            return assemble(cores, c, splits)
        results = []
        for low, high in splits:
            out = blank((n_z, piece_rows, n_f, n_c, high - low), F32)
            for e, piece in enumerate(cores):
                update = jnp.transpose(piece[..., low:high].astype(F32), (0, 2, 1, 3))
                out = lax.dynamic_update_index_in_dim(out, update, c ^ e, 3)
            results.append(out.reshape(shard, n_t * (high - low)))
        return results

    totals = {}

    def finish(name, function, *args):
        def get():
            if name not in totals:
                made = function(*args)
                totals[name] = made if isinstance(made, (list, tuple)) else [made]
            return totals[name]

        return get

    down_done = finish("down", finish_rows, sum_down)
    gate_done = finish("gate", finish_columns, sum_gate, [(0, hidden)])
    up_done = finish("up", finish_columns, sum_up, [(0, hidden)])
    out_done = finish("out", finish_rows, sum_out)
    splits = [(0, q_width), (q_width, q_width + kv_width), (q_width + kv_width, qkv_width)]
    qkv_done = finish("qkv", finish_columns, sum_qkv, splits)

    def slot(which, step):
        return which * n_z + min(step, n_z - 1)

    run_sums(
        sum_down,
        [sum_gate, sum_up, sum_out, sum_qkv],
        {
            slot(1, 3): lambda: [grad_kv],
            slot(2, 1): lambda: [grad_qkv],
            slot(2, 2): lambda: [grad_w_qkv, h_one_parts],
            slot(3, 0): down_done,
            slot(3, 2): gate_done,
            slot(4, 2): lambda: [*up_done(), gain_grads],
            slot(4, 3): out_done,
        },
    )
    total_down, total_gate, total_up, total_out = (
        done()[0] for done in (down_done, gate_done, up_done, out_done)
    )
    total_query, total_key, total_value = qkv_done()
    return (
        mixed.reshape(tokens.shape),
        grad_tokens.reshape(tokens.shape),
        gain_grads[0],
        total_query,
        total_key,
        total_value,
        total_out,
        gain_grads[1],
        total_gate,
        total_up,
        total_down,
    )


def solution(mesh):
    n_ctx, n_fsdp = mesh.shape["ctx"], mesh.shape["fsdp"]
    n_core = KEY_VALUE_HEADS // n_fsdp
    inner = Mesh(
        np.asarray(mesh.devices).reshape(n_ctx // n_core, n_core, n_fsdp), ("z", "core", "f")
    )
    ctx = ("z", "core")
    return jax.shard_map(
        per_device,
        mesh=inner,
        in_specs=(
            P("f", ctx, None, None, None),
            P("f", ctx, None, None),
            P("f"),
            P("f", None),
            P("f", None),
            P("f", None),
            P("f", None),
            P("f"),
            P("f", None),
            P("f", None),
            P("f", None),
            P("f", ctx, None, None, None),
        ),
        out_specs=(
            P("f", ctx, None, None, None),
            P("f", ctx, None, None, None),
            P("f"),
            P("f", None),
            P("f", None),
            P("f", None),
            P("f", None),
            P("f"),
            P("f", None),
            P("f", None),
            P("f", None),
        ),
        check_vma=False,
    )
```
